128 devices in a mesh: group: 4 (over y), dev: 32 (over z, x, core).
Axes of the slice: x: 4, y: 4, z: 4, core: 2. Of those that a mesh axis runs over, the one named last changes fastest.
Arguments:
- particles: float32 [4, 16384, 128], P(None, ('group', 'dev')), may hold values from -0.95 to 0.95
- counts: int32 [16384], P(('group', 'dev')), may hold values from 1 to 128, as said below
- upward: float32 [8, 36, 36], replicated, may hold values from -0.375 to 0.375
- downward: float32 [8, 36, 36], replicated, may hold values from -0.75 to 0.75
- translate: float32 [3, 36, 36, 316], replicated, may hold values from -0.0068359375 to 0.0068359375
- far_send: int32 [128, 128, 16], P(('group', 'dev')), may hold values from -1 to 127, as said below
- mid_send: int32 [128, 128, 4], P(('group', 'dev')), may hold values from -1 to 15, as said below
- top_send: int32 [128, 4, 4], P(('group', 'dev')), may hold values from -1 to 63, as said below
- near_send: int32 [128, 128, 8], P(('group', 'dev')), may hold values from -1 to 127, as said below
- far_lists: int32 [316, 16384], P(None, ('group', 'dev')), may hold values from -1 to 2175, as said below
- mid_lists: int32 [316, 2048], P(None, ('group', 'dev')), may hold values from -1 to 527, as said below
- top_lists: int32 [316, 256], P(None, ('group', 'dev')), may hold values from -1 to 79, as said below
- near_lists: int32 [26, 16384], P(None, ('group', 'dev')), may hold values from 0 to 1151, as said below
Outputs:
- potential: float32 [16384, 128], P(('group', 'dev'))
The draws below stay inside these ranges and needn't reach their ends.
Inputs may be any that keep to these rules, and one draw needn't show every extreme that they name: `counts`: every draw has leaves with 128 particles. `far_send`: row s, column r holds leaves of device s in its first slots and -1 after them; every device fills all 16 slots towards the next rank (wrapping) and at least half of them towards every rank. `mid_send`: as far_send, with middle-level boxes of the sender and 4 slots. `top_send`: entry (s, h, c) indexes the top-level boxes of the sender's group; filled slots come first; every device fills all 4 slots towards the next group (wrapping) and at least half of them towards every group. `near_send`: as far_send, with 8 slots. `far_lists`: slot j stands for the j-th offset of [-3, 3]^3 without [-1, 1]^3 in lexicographic order; it is -1 exactly where that offset leaves the parents' neighbourhood (floor((parity + offset) / 2) outside [-1, 1] in a coordinate, parities the bits of t mod 8 as x + 2 y + 4 z); other entries index leaf_sources of the owner and never an empty received slot. `mid_lists`: as far_lists, for middle-level boxes and mid_sources. `top_lists`: as far_lists, for top-level boxes and top_sources. `near_lists`: entries index near_sources of the owner and never an empty received slot.
All inputs are finite; a program needn't handle non-finite values.
Results may differ from the reference program's by a relative error of at most 0.0003.
Values sent between devices are 32-bit elements; how exact they have to be, the bound alone decides.
No kernel may reach another device: no remote copies, remote signals or barrier semaphores. Data moves between devices by JAX's collectives and lax.ppermute only.
A program may use at most 128 MiB of HBM per device.

```python
import math
import jax
import jax.numpy as jnp
import numpy as np
from jax import lax

ORDER = 6
TERMS = 36
OFFS = 316
NEAR = 26
PMAX = 128
LEAF_DEV = 128
CAP7 = 16
CAP6 = 4
CAP5 = 4
NCAP = 8
RANKS = 128
MID_DEV = 16
TOP_DEV = 2
GROUP_TOPS = 64
TOTAL7 = 16384
N_GROUP = 4
N_DEV = 32


def offset_presence():
    present_rows = []
    for octant in range(8):
        parities = (octant & 1, octant >> 1 & 1, octant >> 2 & 1)
        present_row = []
        for step_x in range(-3, 4):
            for step_y in range(-3, 4):
                for step_z in range(-3, 4):
                    if max(abs(step_x), abs(step_y), abs(step_z)) < 2:
                        continue
                    inside = True
                    for parity, offset in zip(parities, (step_x, step_y, step_z)):
                        parent_step = (parity + offset) // 2
                        if parent_step < -1 or parent_step > 1:
                            inside = False
                    present_row.append(inside)
        present_rows.append(present_row)
    return np.array(present_rows, dtype=bool).T


def cycle_full():
    senders = jnp.arange(RANKS)[:, None]
    targets = jnp.arange(RANKS)[None, :]
    return (targets - senders) % RANKS == 1


def group_full():
    senders = jnp.arange(RANKS)[:, None]
    targets = jnp.arange(N_GROUP)[None, :]
    return targets == (senders // N_DEV + 1) % N_GROUP


def pair_counts(key, salt, receivers, capacity, full_mask):
    drawn_counts = jax.random.randint(jax.random.fold_in(key, salt), (RANKS, receivers), (capacity + 1) // 2, capacity + 1)
    return jnp.where(full_mask, capacity, drawn_counts)


def send_picks(key, counts, capacity, box_count):
    box_picks = jax.random.randint(key, counts.shape + (capacity,), 0, box_count)
    return jnp.where(jnp.arange(capacity) < counts[..., None], box_picks, -1).astype(jnp.int32)


def make_lists(key, counts, box_count, capacity, columns, present_all):
    total_boxes = box_count * RANKS
    target = jnp.arange(total_boxes)
    receiver = target // box_count
    subkeys = jax.random.split(key, 4)
    remote = jax.random.randint(subkeys[0], (columns, total_boxes), 0, 4) == 0
    local_pick = jax.random.randint(subkeys[1], (columns, total_boxes), 0, box_count)
    sender = jax.random.randint(subkeys[2], (columns, total_boxes), 0, RANKS)
    slot_limit = counts[sender, receiver[None, :]]
    slot_pick = jax.random.randint(subkeys[3], (columns, total_boxes), 0, slot_limit)
    remote_pick = box_count + sender * capacity + slot_pick
    chosen = jnp.where(remote, remote_pick, local_pick)
    if present_all:
        return chosen.astype(jnp.int32)
    present = jnp.asarray(offset_presence())[:, target % 8]
    return jnp.where(present, chosen, -1).astype(jnp.int32)


def draw_counts(key, part):
    key = jax.random.fold_in(key, 10)
    subkeys = jax.random.split(key, 2)
    drawn_counts = jax.random.randint(subkeys[0], (TOTAL7,), 1, PMAX + 1)
    full_leaf = jax.random.randint(subkeys[1], (TOTAL7,), 0, 16) == 0
    return jnp.where(full_leaf, PMAX, drawn_counts).astype(jnp.int32)


def draw_far_send(key, part):
    counts = pair_counts(key, 1, RANKS, CAP7, cycle_full())
    key = jax.random.fold_in(key, 11)
    return send_picks(key, counts, CAP7, LEAF_DEV)


def draw_mid_send(key, part):
    counts = pair_counts(key, 2, RANKS, CAP6, cycle_full())
    key = jax.random.fold_in(key, 12)
    return send_picks(key, counts, CAP6, MID_DEV)


def draw_top_send(key, part):
    counts = pair_counts(key, 3, N_GROUP, CAP5, group_full())
    key = jax.random.fold_in(key, 13)
    return send_picks(key, counts, CAP5, GROUP_TOPS)


def draw_near_send(key, part):
    counts = pair_counts(key, 4, RANKS, NCAP, cycle_full())
    key = jax.random.fold_in(key, 14)
    return send_picks(key, counts, NCAP, LEAF_DEV)


def draw_far_lists(key, part):
    counts = pair_counts(key, 1, RANKS, CAP7, cycle_full())
    key = jax.random.fold_in(key, 21)
    return make_lists(key, counts, LEAF_DEV, CAP7, OFFS, False)


def draw_mid_lists(key, part):
    counts = pair_counts(key, 2, RANKS, CAP6, cycle_full())
    key = jax.random.fold_in(key, 22)
    return make_lists(key, counts, MID_DEV, CAP6, OFFS, False)


def draw_near_lists(key, part):
    counts = pair_counts(key, 4, RANKS, NCAP, cycle_full())
    key = jax.random.fold_in(key, 24)
    return make_lists(key, counts, LEAF_DEV, NCAP, NEAR, True)


def draw_top_lists(key, part):
    counts = pair_counts(key, 3, N_GROUP, CAP5, group_full())
    key = jax.random.fold_in(key, 23)
    total_boxes = TOP_DEV * RANKS
    target = jnp.arange(total_boxes)
    receiver = target // TOP_DEV
    group_index = receiver // N_DEV
    member = receiver % N_DEV
    subkeys = jax.random.split(key, 4)
    remote = jax.random.randint(subkeys[0], (OFFS, total_boxes), 0, 4) == 0
    local_pick = jax.random.randint(subkeys[1], (OFFS, total_boxes), 0, GROUP_TOPS)
    source_group = jax.random.randint(subkeys[2], (OFFS, total_boxes), 0, N_GROUP)
    slot_limit = counts[source_group * N_DEV + member[None, :], group_index[None, :]]
    slot_pick = jax.random.randint(subkeys[3], (OFFS, total_boxes), 0, slot_limit)
    remote_pick = GROUP_TOPS + source_group * CAP5 + slot_pick
    chosen = jnp.where(remote, remote_pick, local_pick)
    present = jnp.asarray(offset_presence())[:, target % 8]
    return jnp.where(present, chosen, -1).astype(jnp.int32)


def steps_of(own_key, dims, shards, least, largest):
    def one(dim, blocks):
        heights = jax.random.uniform(jax.random.fold_in(jax.random.fold_in(own_key, 6), dim), (blocks,), jnp.float32, least / len(shards), largest / len(shards))
        return jnp.repeat(jnp.exp(heights), dims[dim] // blocks).reshape((-1,) + (1,) * (len(dims) - dim - 1))

    level = one(*shards[0])
    for cut in shards[1:]:
        level = level * one(*cut)
    return level


def scatter_about(key, shape, scale, bound, kind=jnp.bfloat16):
    values = scale * jax.random.normal(key, shape, jnp.float32)
    return jnp.clip(values, min=-bound, max=bound).astype(kind)


def setup_inputs(seed: int = 0) -> dict:
    arg_keys = jax.random.split(jax.random.key(seed), 14)
    return {
        "particles": jnp.clip(jax.random.uniform(arg_keys[0], (4, TOTAL7, PMAX), jnp.float32, -0.95, 0.95) * steps_of(arg_keys[0], (4, TOTAL7, PMAX), ((1, 128),), -0.4, 0.0), -0.95, 0.95),
        "counts": draw_counts(jax.random.fold_in(arg_keys[13], 71), 0),
        "upward": scatter_about(arg_keys[2], (8, TERMS, TERMS), (8 * TERMS) ** -0.5, 0.375, jnp.float32),
        "downward": scatter_about(arg_keys[3], (8, TERMS, TERMS), (2 * TERMS) ** -0.5, 0.75, jnp.float32),
        "translate": scatter_about(arg_keys[4], (3, TERMS, TERMS, OFFS), (72 * TERMS * OFFS) ** -0.5, 0.0068359375, jnp.float32),
        "far_send": draw_far_send(jax.random.fold_in(arg_keys[13], 71), 0),
        "mid_send": draw_mid_send(jax.random.fold_in(arg_keys[13], 71), 0),
        "top_send": draw_top_send(jax.random.fold_in(arg_keys[13], 71), 0),
        "near_send": draw_near_send(jax.random.fold_in(arg_keys[13], 71), 0),
        "far_lists": draw_far_lists(jax.random.fold_in(arg_keys[13], 71), 0),
        "mid_lists": draw_mid_lists(jax.random.fold_in(arg_keys[13], 71), 0),
        "top_lists": draw_top_lists(jax.random.fold_in(arg_keys[13], 71), 0),
        "near_lists": draw_near_lists(jax.random.fold_in(arg_keys[13], 71), 0),
    }


SOFTEN = 0.01

def harmonics(offsets):
    coord_x = offsets[0]
    coord_y = offsets[1]
    coord_z = offsets[2]
    radius_sq = coord_x * coord_x + coord_y * coord_y + coord_z * coord_z
    real_part = {(0, 0): jnp.ones_like(coord_x)}
    imag_part = {(0, 0): jnp.zeros_like(coord_x)}
    for degree in range(1, ORDER):
        prior_re = real_part[degree - 1, degree - 1]
        prior_im = imag_part[degree - 1, degree - 1]
        real_part[degree, degree] = (coord_x * prior_re - coord_y * prior_im) / (2.0 * degree)
        imag_part[degree, degree] = (coord_x * prior_im + coord_y * prior_re) / (2.0 * degree)
        for column in range(degree):
            upper_re = (2.0 * degree - 1.0) * coord_z * real_part[degree - 1, column]
            upper_im = (2.0 * degree - 1.0) * coord_z * imag_part[degree - 1, column]
            if column <= degree - 2:
                upper_re = upper_re - radius_sq * real_part[degree - 2, column]
                upper_im = upper_im - radius_sq * imag_part[degree - 2, column]
            factor = 1.0 / ((degree + column) * (degree - column))
            real_part[degree, column] = upper_re * factor
            imag_part[degree, column] = upper_im * factor
    pieces = []
    for degree in range(ORDER):
        for column in range(degree + 1):
            weight = math.sqrt(math.factorial(degree - column) * math.factorial(degree + column))
            pieces.append(weight * real_part[degree, column])
            if column > 0:
                pieces.append(weight * imag_part[degree, column])
    return jnp.stack(pieces, axis=0)

def near_offsets():
    shifts = []
    for step_x in (-1, 0, 1):
        for step_y in (-1, 0, 1):
            for step_z in (-1, 0, 1):
                if step_x != 0 or step_y != 0 or step_z != 0:
                    shifts.append((step_x, step_y, step_z))
    return np.array(shifts, dtype=np.float32)

def pair_field(targets, sources, displace, exclude):
    diff_x = targets[0][:, :, None] - sources[0][:, None, :] - displace[0]
    diff_y = targets[1][:, :, None] - sources[1][:, None, :] - displace[1]
    diff_z = targets[2][:, :, None] - sources[2][:, None, :] - displace[2]
    inverse = lax.rsqrt(diff_x * diff_x + diff_y * diff_y + diff_z * diff_z + SOFTEN)
    weighted = sources[3][:, None, :] * inverse
    if exclude:
        slot_count = targets.shape[2]
        same_slot = jnp.arange(slot_count)[:, None] == jnp.arange(slot_count)[None, :]
        weighted = jnp.where(same_slot[None], 0.0, weighted)
    return lax.optimization_barrier(jnp.sum(weighted, axis=2))

def translate_level(operator, source_table, source_lists):
    clipped = jnp.maximum(source_lists, 0)
    picked = jnp.take(source_table, clipped, axis=1)
    picked = jnp.where(source_lists[None] >= 0, picked, 0.0)
    term_count = operator.shape[0]
    return jnp.dot(operator.reshape(term_count, -1), picked.reshape(-1, source_lists.shape[1]), precision=lax.Precision.HIGHEST)

def upward_pass(upward, moments):
    term_count, box_count = moments.shape
    grouped = moments.reshape(term_count, box_count // 8, 8)
    return jnp.einsum('oik,kqo->iq', upward, grouped, precision=lax.Precision.HIGHEST)

def downward_pass(downward, parents, children):
    term_count, box_count = parents.shape
    spread = jnp.einsum('oik,kq->iqo', downward, parents, precision=lax.Precision.HIGHEST)
    return children + spread.reshape(term_count, box_count * 8)

def reference(particles, counts, upward, downward, translate, far_send, mid_send, top_send, near_send, far_lists, mid_lists, top_lists, near_lists):
    rank_count = N_GROUP * N_DEV
    slot_count = particles.shape[2]
    mid_dev = LEAF_DEV // 8
    top_dev = LEAF_DEV // 64
    group_tops = N_DEV * top_dev
    filled = jnp.arange(slot_count, dtype=jnp.int32)[None, :] < counts[:, None]
    charge = jnp.where(filled, particles[3], 0.0)
    packed = jnp.concatenate([particles[:3], charge[None]], axis=0)
    basis_values = harmonics(particles[:3])
    leaf_moments = jnp.einsum('kbp,bp->kb', basis_values, charge, precision=lax.Precision.HIGHEST)
    mid_moments = upward_pass(upward, leaf_moments)
    top_moments = upward_pass(upward, mid_moments)
    senders = jnp.arange(rank_count, dtype=jnp.int32)
    shifts = near_offsets()

    def received(moments, sends, rank_index, box_count):
        send_rows = sends[:, rank_index, :]
        box_ids = senders[:, None] * box_count + jnp.maximum(send_rows, 0)
        picked = jnp.take(moments, box_ids, axis=1)
        picked = jnp.where(send_rows[None] >= 0, picked, 0.0)
        return picked.reshape(moments.shape[0], -1)

    def one_rank(rank_index):
        leaf_start = rank_index * LEAF_DEV
        mid_start = rank_index * mid_dev
        top_start = rank_index * top_dev
        own_leaves = lax.dynamic_slice_in_dim(leaf_moments, leaf_start, LEAF_DEV, 1)
        leaf_table = jnp.concatenate([own_leaves, received(leaf_moments, far_send, rank_index, LEAF_DEV)], axis=1)
        leaf_local = translate_level(translate[0], leaf_table, lax.dynamic_slice_in_dim(far_lists, leaf_start, LEAF_DEV, 1))
        own_mids = lax.dynamic_slice_in_dim(mid_moments, mid_start, mid_dev, 1)
        mid_table = jnp.concatenate([own_mids, received(mid_moments, mid_send, rank_index, mid_dev)], axis=1)
        mid_local = translate_level(translate[1], mid_table, lax.dynamic_slice_in_dim(mid_lists, mid_start, mid_dev, 1))
        group_index = rank_index // N_DEV
        member = rank_index % N_DEV
        group_table = lax.dynamic_slice_in_dim(top_moments, group_index * group_tops, group_tops, 1)
        group_ids = jnp.arange(N_GROUP, dtype=jnp.int32)
        send_rows = top_send[group_ids * N_DEV + member, group_index, :]
        box_ids = group_ids[:, None] * group_tops + jnp.maximum(send_rows, 0)
        top_in = jnp.take(top_moments, box_ids, axis=1)
        top_in = jnp.where(send_rows[None] >= 0, top_in, 0.0).reshape(top_moments.shape[0], -1)
        top_table = jnp.concatenate([group_table, top_in], axis=1)
        top_local = translate_level(translate[2], top_table, lax.dynamic_slice_in_dim(top_lists, top_start, top_dev, 1))
        mid_total = downward_pass(downward, top_local, mid_local)
        leaf_total = downward_pass(downward, mid_total, leaf_local)
        own_basis = lax.dynamic_slice_in_dim(basis_values, leaf_start, LEAF_DEV, 1)
        far_field = jnp.einsum('kb,kbp->bp', leaf_total, own_basis, precision=lax.Precision.HIGHEST)
        own_packed = lax.dynamic_slice_in_dim(packed, leaf_start, LEAF_DEV, 1)
        near_rows = near_send[:, rank_index, :]
        near_ids = senders[:, None] * LEAF_DEV + jnp.maximum(near_rows, 0)
        near_in = jnp.take(packed, near_ids, axis=1)
        near_in = jnp.where(near_rows[None, :, :, None] >= 0, near_in, 0.0)
        near_table = jnp.concatenate([own_packed, near_in.reshape(4, -1, slot_count)], axis=1)
        own_near = lax.dynamic_slice_in_dim(near_lists, leaf_start, LEAF_DEV, 1)
        near_field = pair_field(own_packed, own_packed, (0.0, 0.0, 0.0), True)
        for slot_index in range(NEAR):
            sources = jnp.take(near_table, own_near[slot_index], axis=1)
            displace = tuple((2.0 * float(value) for value in shifts[slot_index]))
            near_field = near_field + pair_field(own_packed, sources, displace, False)
        own_filled = lax.dynamic_slice_in_dim(filled, leaf_start, LEAF_DEV, 0)
        return jnp.where(own_filled, near_field + far_field, 0.0)
    blocks = lax.map(one_rank, senders)
    return blocks.reshape(rank_count * LEAF_DEV, slot_count)
```

```python
import math

import jax
import jax.numpy as jnp
import numpy as np
from jax import lax
from jax.experimental import pallas as pl
from jax.experimental.pallas import tpu as pltpu
from jax.sharding import PartitionSpec as P

ORDER = 6
TERMS = 36
OFFS = 316
SOFTEN = 0.01
LEAVES = 128
SLOTS = 128
RANKS = 128
AXES = ("group", "dev")
F32 = jnp.float32
BF16 = jnp.bfloat16
I32 = jnp.int32
HIGH = lax.Precision.HIGHEST
VMEM = pltpu.VMEM
SMEM = pltpu.SMEM
MIB = 1 << 20
CHUNK = 4
ROWS = 64
NEAR_PAD = 28
DEPTH = 4


def harmonics(coord_x, coord_y, coord_z):
    radius_sq = coord_x * coord_x + coord_y * coord_y + coord_z * coord_z
    real_part = {(0, 0): jnp.ones_like(coord_x)}
    imag_part = {}
    for degree in range(1, ORDER):
        scale = 1.0 / (2.0 * degree)
        if degree == 1:
            real_part[1, 1] = coord_x * scale
            imag_part[1, 1] = coord_y * scale
        else:
            prior_re = real_part[degree - 1, degree - 1]
            prior_im = imag_part[degree - 1, degree - 1]
            real_part[degree, degree] = (coord_x * prior_re - coord_y * prior_im) * scale
            imag_part[degree, degree] = (coord_x * prior_im + coord_y * prior_re) * scale
        for column in range(degree):
            factor = 1.0 / ((degree + column) * (degree - column))
            lead = ((2.0 * degree - 1.0) * factor) * coord_z
            for part in (real_part, imag_part):
                if (degree - 1, column) not in part:
                    continue
                value = lead * part[degree - 1, column]
                if column <= degree - 2:
                    value = value - (radius_sq * factor) * part[degree - 2, column]
                part[degree, column] = value
    pieces = []
    for degree in range(ORDER):
        for column in range(degree + 1):
            weight = math.sqrt(math.factorial(degree - column) * math.factorial(degree + column))
            pieces.append(weight * real_part[degree, column])
            if column > 0:
                pieces.append(weight * imag_part[degree, column])
    return pieces


def near_offsets():
    shifts = []
    for step_x in (-1, 0, 1):
        for step_y in (-1, 0, 1):
            for step_z in (-1, 0, 1):
                if step_x != 0 or step_y != 0 or step_z != 0:
                    shifts.append((step_x, step_y, step_z))
    return shifts


def far_groups():
    offsets = []
    for step_x in range(-3, 4):
        for step_y in range(-3, 4):
            for step_z in range(-3, 4):
                if max(abs(step_x), abs(step_y), abs(step_z)) >= 2:
                    offsets.append((step_x, step_y, step_z))
    groups = {}
    for j, offset in enumerate(offsets):
        mask, value = 0, 0
        for axis in range(3):
            if abs(offset[axis]) == 3:
                mask |= 1 << axis
                if offset[axis] == -3:
                    value |= 1 << axis
        key = tuple(abs(v) if abs(v) == 3 else v for v in offset)
        groups.setdefault(key, []).append((j, mask, value))
    return sorted(groups.values(), key=len)


GROUPS = far_groups()


def split3(value):
    high = value.astype(BF16).astype(F32)
    rest = value - high
    mid = rest.astype(BF16).astype(F32)
    return high, mid, rest - mid


def iota(shape, dim):
    return lax.broadcasted_iota(I32, shape, dim)


def pack_kernel(send, part, cnt, tab, out):
    filled = jnp.where(iota((SLOTS, LEAVES), 0) < cnt[...], 1.0, 0.0).T
    comps = [part[0], part[1], part[2], jnp.where(filled > 0.5, part[3], 0.0)]
    for a in range(4):
        tab[pl.ds(a, LEAVES, stride=8), :] = comps[a]
        tab[pl.ds(a + 4, LEAVES, stride=8), :] = comps[a]
    upper = iota((8, 128), 0) < 4

    def body(r, carry):
        for k in range(4):
            first = jnp.maximum(send[r, 2 * k], 0)
            second = jnp.maximum(send[r, 2 * k + 1], 0)
            tile0 = tab[pl.ds(pl.multiple_of(first * 8, 8), 8), :]
            tile1 = tab[pl.ds(pl.multiple_of(second * 8, 8), 8), :]
            out[r, 8 * k : 8 * k + 8, :] = jnp.where(upper, tile0, tile1)
        return carry

    lax.fori_loop(0, RANKS, body, 0, unroll=4)


def pack_near(near_rows, particles, cnt):
    return pl.pallas_call(
        pack_kernel,
        out_shape=(
            jax.ShapeDtypeStruct((LEAVES * 8, 128), F32),
            jax.ShapeDtypeStruct((RANKS, 32, 128), F32),
        ),
        in_specs=[pl.BlockSpec(memory_space=SMEM), pl.BlockSpec(memory_space=VMEM), pl.BlockSpec(memory_space=VMEM)],
        out_specs=(pl.BlockSpec(memory_space=VMEM), pl.BlockSpec(memory_space=VMEM)),
        compiler_params=pltpu.CompilerParams(vmem_limit_bytes=32 * MIB),
        cost_estimate=pl.CostEstimate(flops=3_000_000, bytes_accessed=3 * MIB, transcendentals=0),
        name="pack_near",
    )(near_rows, particles, cnt)


def nt(left, right):
    return lax.dot_general(left, right, (((1,), (1,)), ((), ())), precision=HIGH, preferred_element_type=F32)


def moments_kernel(part, cnt, idx3, tops, upward, sent, leaf_out, mid_out, xs, table):
    filled = iota((SLOTS, LEAVES), 0) < cnt[...]
    for a in range(3):
        xs[a] = part[a].T
    xs[3] = jnp.where(filled, part[3].T, 0.0)

    def chunk(c, acc):
        rows = pl.ds(pl.multiple_of(c * 8, 8), 8)
        charge = xs[3, rows, :]
        basis = harmonics(xs[0, rows, :], xs[1, rows, :], xs[2, rows, :])
        return tuple(old + charge * value for old, value in zip(acc, basis))

    zero = jnp.zeros((8, 128), F32)
    acc = lax.fori_loop(0, SLOTS // 8, chunk, (zero,) * TERMS)
    rows = [jnp.sum(value, axis=0, keepdims=True) for value in acc]
    leaf = jnp.concatenate(rows + [jnp.zeros((4, 128), F32)], axis=0)
    leaf_out[...] = leaf
    table[...] = jnp.zeros((256, 128), F32)
    table[0:128, :] = jnp.concatenate([leaf, jnp.zeros((88, 128), F32)], axis=0).T
    mid = jnp.zeros((16, TERMS), F32)
    for o in range(8):
        mid = mid + nt(table[pl.ds(o, 16, stride=8), :][:, :TERMS], upward[o])
    table[128:144, 0:TERMS] = mid
    top = jnp.zeros((2, TERMS), F32)
    for o in range(8):
        top = top + nt(table[pl.ds(128 + o, 2, stride=8), :][:, :TERMS], upward[o])
    table[144:146, 0:TERMS] = top
    table[160:168, :] = tops[...]
    mid_wide = jnp.concatenate([table[128:144, :], jnp.zeros((112, 128), F32)], axis=0)
    mid_out[...] = mid_wide.T[0:40]
    weights = []
    for a in range(3):
        values = table[...] if a == 0 else pltpu.roll(table[...], 40 * a, 1)
        high, middle, low = split3(values)
        weights.append((jnp.concatenate([high, middle], axis=1).astype(BF16), low.astype(BF16)))
    lane = iota((128, 256), 1)

    def pick(e, carry):
        rows = pl.ds(pl.multiple_of(e * 128, 128), 128)
        columns = idx3[rows, :]
        total = jnp.zeros((128, 128), F32)
        for a in range(3):
            hot = jnp.where(columns[:, a : a + 1] == lane, 1.0, 0.0).astype(BF16)
            both = jnp.dot(hot, weights[a][0], preferred_element_type=F32)
            total = total + (both[:, :128] + both[:, 128:]) + jnp.dot(hot, weights[a][1], preferred_element_type=F32)
        sent[rows, :] = total
        return carry

    lax.fori_loop(0, 8, pick, 0)


def moments(particles, cnt, idx3, tops, upward):
    return pl.pallas_call(
        moments_kernel,
        out_shape=(
            jax.ShapeDtypeStruct((RANKS * 8, 128), F32),
            jax.ShapeDtypeStruct((40, 128), F32),
            jax.ShapeDtypeStruct((40, 128), F32),
        ),
        in_specs=[pl.BlockSpec(memory_space=VMEM)] * 5,
        out_specs=(pl.BlockSpec(memory_space=VMEM),) * 3,
        scratch_shapes=[VMEM((4, SLOTS, LEAVES), F32), VMEM((256, 128), F32)],
        compiler_params=pltpu.CompilerParams(vmem_limit_bytes=32 * MIB),
        cost_estimate=pl.CostEstimate(flops=5_000_000, bytes_accessed=2 * MIB, transcendentals=0),
        name="moments",
    )(particles, cnt, idx3, tops, upward)


def shift_tables():
    scale = np.zeros((32, 8, 128), np.float32)
    add = np.zeros((32, 8, 128), np.float32)
    shifts = near_offsets() + [(0, 0, 0)] * 6
    for j, shift in enumerate(shifts):
        for a in range(3):
            scale[j, a] = 1.0
            scale[j, a + 4] = 1.0
            add[j, a] = 2.0 * shift[a]
            add[j, a + 4] = 2.0 * shift[a]
        add[j, 3] = 1.0
    return scale.reshape(256, 128)[:8], add.reshape(256, 128)


def source_matrix(tile, scale, add, upper):
    moved = tile * scale + add
    values = jnp.where(upper, moved, moved * moved)
    high, middle, low = split3(values)
    return jnp.concatenate([high, high, middle, high, middle, low], axis=0).astype(BF16)


def near_kernel(first, lists, meta, total, tab_in, scale_in, add_in, target_in, prev, field, target_out, tab, bufs, mats, acc):
    upper = iota((8, 128), 0) < 4
    scale = scale_in[...]
    sub8 = iota((8, 128), 0)
    if first:
        n_tab = LEAVES
        tab[0 : 8 * n_tab, :] = tab_in[...]
        target = target_out

        def build(b, carry):
            tile = tab_in[pl.ds(pl.multiple_of(b * 8, 8), 8), :]
            square = jnp.where(upper & (sub8 < 3), tile * tile, 0.0)
            norm = jnp.sum(square, axis=0, keepdims=True) + SOFTEN
            values = jnp.where(sub8 < 3, -2.0 * tile, jnp.where(sub8 == 3, norm, jnp.where(sub8 < 7, 1.0, 0.0)))
            high, middle, low = split3(values)
            wide = jnp.concatenate([high, middle, high, low, middle, high], axis=0)
            target[pl.ds(pl.multiple_of(b * 128, 128), 128), :] = wide.T.astype(BF16)
            return carry

        lax.fori_loop(0, LEAVES, build, 0, unroll=2)
        target[LEAVES * 128 :, :] = jnp.zeros((128, 48), BF16)
    else:
        n_tab = RANKS * 8
        target = target_in

        def build(s, carry):
            for k in range(4):
                tile = tab_in[s, 8 * k : 8 * k + 8, :]
                turned = pltpu.roll(tile, 4, 0)
                base = pl.multiple_of(s * 64 + k * 16, 16)
                tab[pl.ds(base, 8), :] = jnp.where(upper, tile, turned)
                tab[pl.ds(base + 8, 8), :] = jnp.where(upper, turned, tile)
            return carry

        lax.fori_loop(0, RANKS, build, 0, unroll=2)
    tab[8 * n_tab : 8 * n_tab + 8, :] = jnp.zeros((8, 128), F32)

    def parts(unit):
        return unit & 255, lax.shift_right_logical(unit, 8) & 1, lax.shift_right_logical(unit, 9)

    def entry(b, ch, l):
        word = lists[ch * CHUNK + l, b]
        leaf = lax.shift_right_logical(word, 5)
        return pl.multiple_of(leaf * 8, 8), pl.multiple_of((word & 31) * 8, 8)

    def prepare(unit, mat):
        b, _, ch = parts(unit)
        for l in range(CHUNK):
            place, slot = entry(b, ch, l)
            mat[:, 128 * l : 128 * l + 128] = source_matrix(tab[pl.ds(place, 8), :], scale, add_in[pl.ds(slot, 8), :], upper)

    def distances(unit, mat, buf):
        b, rg, _ = parts(unit)
        left = target[pl.ds(pl.multiple_of(b * 128 + rg * ROWS, ROWS), ROWS), :]
        for pair in range(CHUNK // 2):
            lanes = slice(256 * pair, 256 * pair + 256)
            buf[:, lanes] = jnp.dot(left, mat[:, lanes], preferred_element_type=F32)

    def gather(unit, buf):
        b, rg, ch = parts(unit)
        part = None
        for l in range(CHUNK):
            place, _ = entry(b, ch, l)
            charge = tab[pl.ds(place, 8), :][3:4]
            term = lax.rsqrt(buf[:, 128 * l : 128 * l + 128]) * charge
            part = term if part is None else part + term
        rows = pl.ds(pl.multiple_of(b * 128 + rg * ROWS, ROWS), ROWS)
        acc[rows, :] = acc[rows, :] + part

    def following(unit):
        b, rg, ch = parts(unit)
        wrap = ch + 1 >= meta[0, b]
        ch = jnp.where(wrap, 0, ch + 1)
        rg = jnp.where(wrap, rg + 1, rg)
        done = rg >= meta[1, b]
        rg = jnp.where(done, 0, rg)
        b = jnp.minimum(jnp.where(done, b + 1, b), LEAVES)
        return b + rg * 256 + ch * 512

    if first:
        same = iota((128, 128), 0) == iota((128, 128), 1)

        def self_pairs(i, carry):
            for l in range(4):
                b = i * 4 + l
                tile = tab[pl.ds(pl.multiple_of(b * 8, 8), 8), :]
                mat = source_matrix(tile, scale, add_in[31 * 8 : 32 * 8, :], upper)
                rows = pl.ds(pl.multiple_of(b * 128, 128), 128)
                square = jnp.dot(target[rows, :], mat, preferred_element_type=F32)
                acc[rows, :] = jnp.where(same, 0.0, lax.rsqrt(square) * tile[3:4])
            return carry

        lax.fori_loop(0, LEAVES // 4, self_pairs, 0)
    else:
        acc[...] = jnp.zeros(acc.shape, F32)
    acc[LEAVES * 128 :, :] = jnp.zeros((128, 128), F32)

    def step(u, units):
        units = list(units)
        for n in range(DEPTH):
            gather(units[n], bufs.at[n])
        for n in range(DEPTH):
            distances(units[DEPTH + n], mats.at[n], bufs.at[n])
        for n in range(DEPTH):
            prepare(units[2 * DEPTH + n], mats.at[n])
        for n in range(DEPTH):
            units.append(following(units[-1]))
        return tuple(units[DEPTH:])

    units = [jnp.int32(LEAVES)] * (2 * DEPTH) + [jnp.int32(0)]
    for n in range(DEPTH - 1):
        units.append(following(units[-1]))
    lax.fori_loop(0, (total[0] + (DEPTH - 1)) // DEPTH + 2, step, tuple(units))

    field[...] = jnp.zeros((128, 128), F32) if prev is None else prev[...]
    lane = iota((128, 128), 1)

    def reduce(i, carry):
        value = field[...]
        for l in range(8):
            b = i * 8 + l
            rows = pl.ds(pl.multiple_of(b * 128, 128), 128)
            value = jnp.where(lane == b, value + jnp.sum(acc[rows, :], axis=1, keepdims=True), value)
        field[...] = value
        return carry

    lax.fori_loop(0, LEAVES // 8, reduce, 0)


def near_pass(lists, meta, total, tab, target=None, prev=None):
    first = target is None
    scale, add = shift_tables()
    n_tab = LEAVES if first else RANKS * 8
    v = pl.BlockSpec(memory_space=VMEM)
    s = pl.BlockSpec(memory_space=SMEM)
    scratch = [
        VMEM((8 * n_tab + 8, 128), F32),
        VMEM((DEPTH, ROWS, 128 * CHUNK), F32),
        VMEM((DEPTH, 48, 128 * CHUNK), BF16),
        VMEM(((LEAVES + 1) * 128, 128), F32),
    ]
    params = pltpu.CompilerParams(vmem_limit_bytes=48 * MIB)
    cost = pl.CostEstimate(flops=30_000_000_000, bytes_accessed=8 * MIB, transcendentals=20_000_000)
    field_type = jax.ShapeDtypeStruct((128, 128), F32)
    if first:

        def kernel(lists, meta, total, tab_in, scale_in, add_in, field, target_out, *rest):
            near_kernel(True, lists, meta, total, tab_in, scale_in, add_in, None, None, field, target_out, *rest)

        return pl.pallas_call(
            kernel,
            out_shape=(field_type, jax.ShapeDtypeStruct(((LEAVES + 1) * 128, 48), BF16)),
            in_specs=[s, s, s, v, v, v],
            out_specs=(v, v),
            scratch_shapes=scratch,
            compiler_params=params,
            cost_estimate=cost,
            name="near_own",
        )(lists, meta, total, tab, jnp.asarray(scale), jnp.asarray(add))

    def kernel(lists, meta, total, tab_in, scale_in, add_in, target_in, prev, field, *rest):
        near_kernel(False, lists, meta, total, tab_in, scale_in, add_in, target_in, prev, field, None, *rest)

    return pl.pallas_call(
        kernel,
        out_shape=field_type,
        in_specs=[s, s, s, v, v, v, v, v],
        out_specs=v,
        scratch_shapes=scratch,
        compiler_params=params,
        cost_estimate=cost,
        name="near_received",
    )(lists, meta, total, tab, jnp.asarray(scale), jnp.asarray(add), target, prev)


def near_tables(near_lists, counts):
    own = near_lists < LEAVES
    before = jnp.cumsum(own.astype(I32), axis=0)
    order = jnp.arange(1, 27, dtype=I32)[:, None]
    slot = jnp.arange(26, dtype=I32)[:, None]
    groups = (counts + (ROWS - 1)) // ROWS
    result = []
    for mine, place, base, dummy in ((own, before - 1, 0, LEAVES), (~own, order - before - 1, LEAVES, RANKS * 8)):
        word = (near_lists - base) * 32 + slot - dummy * 32
        place = jnp.where(mine, place, -1)
        hits = place[None] == jnp.arange(NEAR_PAD, dtype=I32)[:, None, None]
        table = jnp.sum(jnp.where(hits, word[None], 0), axis=1) + dummy * 32
        table = jnp.pad(table, ((0, 0), (0, 8)), constant_values=dummy * 32)
        number = jnp.sum(mine.astype(I32), axis=0)
        chunks = jnp.maximum((number + (CHUNK - 1)) // CHUNK, 1)
        meta = jnp.pad(jnp.stack([chunks, groups]), ((0, 0), (0, 8)), constant_values=1)
        result.append((table, meta, jnp.sum(chunks * groups).reshape(1)))
    return result


def group_table():
    rows = []
    for group in GROUPS:
        rows.append([word for entry in group for word in entry])
    return rows


N1 = sum(len(g) == 1 for g in GROUPS)
N2 = sum(len(g) == 2 for g in GROUPS)
N4 = sum(len(g) == 4 for g in GROUPS)
N8 = sum(len(g) == 8 for g in GROUPS)
MERGED = len(GROUPS)
MERGED_PAD = 192


def group_words():
    words = np.zeros((MERGED_PAD, 8), np.int32)
    for m, group in enumerate(GROUPS):
        for g in range(8):
            j, mask, value = group[min(g, len(group) - 1)]
            words[m, g] = j * 64 + mask * 8 + value
    return words


def far_kernel(
    words, where_am_i, recv, leaf, mid, far_lists, small_lists, operators, downward, part, cnt, near,
    out, rt, merged, wide, small, xs, parents, leaves,
):
    for i in range(8):
        rt[:, 128 * i : 128 * i + 128] = recv[128 * i : 128 * i + 128, :].T

    def two(value):
        high = value.astype(BF16).astype(F32)
        return jnp.concatenate([high, value - high], axis=0).astype(BF16)

    table = two(jnp.concatenate([leaf[...], rt[0:40, :], rt[40:80, :]], axis=1))
    for m, group in enumerate(GROUPS):
        row = far_lists[group[0][0] : group[0][0] + 1, :]
        for j, _, _ in group[1:]:
            row = jnp.maximum(row, far_lists[j : j + 1, :])
        merged[m : m + 1, :] = row
    merged[MERGED:, :] = jnp.full((MERGED_PAD - MERGED, 128), -1, I32)
    index = merged[...]
    rel = index - LEAVES
    slot = rel & 15
    moved = LEAVES + lax.shift_right_logical(slot, 3) * 1024 + lax.shift_right_logical(rel, 4) * 8 + (slot & 7)
    merged[...] = jnp.where(rel >= 0, moved, index)
    lane = iota((40, 128), 1)

    def hot(row, depth):
        width = row.shape[1]
        upper = lax.shift_right_arithmetic(row, 8)
        lower = (row & 255).astype(F32)
        pieces = []
        for c in range((depth + 255) // 256):
            height = min(256, depth - 256 * c)
            target = jnp.where(upper == c, lower, -1.0)
            number = iota((height, width), 0).astype(F32)
            pieces.append(jnp.where(target == number, 1.0, 0.0).astype(BF16))
        return jnp.concatenate(pieces, axis=0)

    def expand(values, m, size):
        for g in range(size):
            word = words[m, g]
            j = lax.shift_right_logical(word, 6)
            keep = (lane & (lax.shift_right_logical(word, 3) & 7)) == (word & 7)
            wide[pl.ds(j, 40, stride=320), :] = jnp.where(keep, values, 0.0)

    def block(first_row, size):
        def body(i, carry):
            m = first_row + 2 * i
            row = jnp.concatenate([merged[pl.ds(m, 1), :], merged[pl.ds(m + 1, 1), :]], axis=1)
            both = jnp.dot(table, hot(row, 2176), preferred_element_type=F32)
            value = both[0:40] + both[40:80]
            expand(value[:, :128], m, size)
            expand(value[:, 128:], m + 1, size)
            return carry

        return body

    lax.fori_loop(0, N1 // 2, block(0, 1), 0)
    lax.fori_loop(0, (N2 + 1) // 2, block(N1, 2), 0)
    lax.fori_loop(0, (N4 + N8) // 2, block(N1 + N2, 8), 0)

    def contract(left, right, dims):
        lh = left.astype(BF16)
        ll = (left - lh.astype(F32)).astype(BF16)
        rh = right.astype(BF16)
        rl = (right - rh.astype(F32)).astype(BF16)
        dot = lambda a, b: lax.dot_general(a, b, (dims, ((), ())), preferred_element_type=F32)
        return dot(lh, rh) + dot(ll, rh) + dot(lh, rl)

    local = jnp.zeros((TERMS, 128), F32)
    for k in range(TERMS):
        local = local + contract(operators[0, :, k, :], wide[320 * k : 320 * k + OFFS, :], ((1,), (0,)))

    table_small = two(jnp.concatenate([mid[...], rt[80:120, :]], axis=1))
    lists = small_lists[...]
    rel = lists - 16
    mid_place = jnp.where(rel >= 0, LEAVES + lax.shift_right_logical(rel, 2) * 8 + (rel & 3), lists)
    me = where_am_i[0]
    group = lax.shift_right_logical(me, 5)
    top_place = jnp.where(lists >= 0, LEAVES + (group * 32 + lax.shift_right_arithmetic(lists, 1)) * 8 + 4 + (lists & 1), -1)
    for h in range(4):
        row = recv[pl.ds((h * 32 + (me & 31)) * 8 + 6, 1), :]
        for c in range(4):
            box = row[:, 120 + c : 121 + c].astype(I32)
            place = LEAVES + (h * 32 + lax.shift_right_arithmetic(box, 1)) * 8 + 4 + (box & 1)
            top_place = jnp.where(lists == 64 + 4 * h + c, place, top_place)
    place = jnp.where(iota(lists.shape, 0) < 16, mid_place, top_place)
    for t in range(18):
        both = jnp.dot(table_small, hot(place[t : t + 1], 1152), preferred_element_type=F32)
        value = both[0:40] + both[40:80]
        for c in range(3):
            small[c, 40 * t : 40 * t + 40, :] = value[:, 128 * c : 128 * c + 128]
    mid_local = jnp.zeros((16, TERMS), F32)
    top_local = jnp.zeros((2, TERMS), F32)

    def every_40th(start, size):
        return jnp.concatenate([small[c, pl.ds(start, size, stride=40), :] for c in range(3)], axis=1)[:, :OFFS]

    for k in range(TERMS):
        dims = ((1,), (1,))
        mid_local = mid_local + contract(every_40th(k, 16), operators[1, :, k, :], dims)
        top_local = top_local + contract(every_40th(640 + k, 2), operators[2, :, k, :], dims)

    for o in range(8):
        parents[pl.ds(o, 2, stride=8), 0:TERMS] = nt(top_local, downward[o])
    mid_total = parents[:, 0:TERMS] + mid_local
    leaves[...] = jnp.zeros((128, 128), F32)
    for o in range(8):
        leaves[pl.ds(o, 16, stride=8), 0:TERMS] = nt(mid_total, downward[o])
    leaves[...] = leaves[...].T
    leaves[0:TERMS, :] = leaves[0:TERMS, :] + local
    for a in range(3):
        xs[a] = part[a].T

    def chunk(c, carry):
        rows = pl.ds(pl.multiple_of(c * 8, 8), 8)
        basis = harmonics(xs[0, rows, :], xs[1, rows, :], xs[2, rows, :])
        total = near[rows, :]
        for k in range(TERMS):
            total = total + leaves[k : k + 1, :] * basis[k]
        xs[3, rows, :] = jnp.where(iota((8, 128), 0) + c * 8 < cnt[...], total, 0.0)
        return carry

    lax.fori_loop(0, SLOTS // 8, chunk, 0)
    out[...] = xs[3].T


def far_pass(where_am_i, recv, leaf, mid, far_lists, small_lists, translate, downward, particles, cnt, near):
    v = pl.BlockSpec(memory_space=VMEM)
    s = pl.BlockSpec(memory_space=SMEM)
    return pl.pallas_call(
        far_kernel,
        out_shape=jax.ShapeDtypeStruct((LEAVES, SLOTS), F32),
        in_specs=[s, s] + [v] * 10,
        out_specs=v,
        scratch_shapes=[
            VMEM((128, 1024), F32),
            VMEM((MERGED_PAD, 128), I32),
            VMEM((40 * 320, 128), F32),
            VMEM((3, 18 * 40, 128), F32),
            VMEM((4, 128, 128), F32),
            VMEM((16, 128), F32),
            VMEM((128, 128), F32),
        ],
        compiler_params=pltpu.CompilerParams(vmem_limit_bytes=48 * MIB),
        cost_estimate=pl.CostEstimate(flops=20_000_000_000, bytes_accessed=10 * MIB, transcendentals=0),
        name="far_pass",
    )(jnp.asarray(group_words()), where_am_i, recv, leaf, mid, far_lists, small_lists, translate, downward, particles, cnt, near)


def local(
    particles,
    counts,
    upward,
    downward,
    translate,
    far_send,
    mid_send,
    top_send,
    near_send,
    far_lists,
    mid_lists,
    top_lists,
    near_lists,
):
    me = lax.axis_index("group") * 32 + lax.axis_index("dev")
    cnt = counts.reshape(1, LEAVES)
    tab, near_out = pack_near(near_send[0], particles, cnt)
    near_in = lax.all_to_all(near_out, AXES, split_axis=0, concat_axis=0, tiled=True)

    far_rows = far_send[0]
    mid_rows = jnp.where(mid_send[0] >= 0, mid_send[0] + 128, -1)
    rank = jnp.arange(RANKS, dtype=I32)[:, None]
    tail = jnp.concatenate([jnp.full((RANKS, 1), 144, I32), jnp.full((RANKS, 1), 145, I32), 160 + rank // 32, jnp.full((RANKS, 1), -1, I32)], axis=1)
    idx3 = jnp.stack([far_rows[:, :8], far_rows[:, 8:], jnp.concatenate([mid_rows, tail], axis=1)], axis=-1)
    tops = jnp.pad(top_send[0].astype(F32), ((0, 4), (40, 84)))
    sent, leaf, mid = moments(particles, cnt, idx3.reshape(RANKS * 8, 3), tops, upward)
    recv = lax.all_to_all(sent.reshape(RANKS, 8, 128), AXES, split_axis=0, concat_axis=0, tiled=True)

    own, received = near_tables(near_lists, counts)
    near, target = near_pass(*own, tab)
    near = near_pass(*received, near_in, target, near)
    small_lists = jnp.pad(jnp.concatenate([mid_lists, top_lists], axis=1).T, ((0, 6), (0, 68)), constant_values=-1)
    return far_pass(
        me.reshape(1), recv.reshape(RANKS * 8, 128), leaf, mid, far_lists, small_lists, translate, downward, particles, cnt, near
    )


def solution(mesh):
    in_specs = (
        P(None, AXES, None),
        P(AXES),
        P(),
        P(),
        P(),
        P(AXES, None, None),
        P(AXES, None, None),
        P(AXES, None, None),
        P(AXES, None, None),
        P(None, AXES),
        P(None, AXES),
        P(None, AXES),
        P(None, AXES),
    )
    return jax.shard_map(local, mesh=mesh, in_specs=in_specs, out_specs=P(AXES, None), check_vma=False)
```

```python
import math

import jax
import jax.numpy as jnp
import numpy as np
from jax import lax
from jax.experimental import pallas as pl
from jax.experimental.pallas import tpu as pltpu
from jax.sharding import PartitionSpec as P

ORDER = 6
TERMS = 36
OFFS = 316
SOFTEN = 0.01
LEAVES = 128
SLOTS = 128
RANKS = 128
AXES = ("group", "dev")
F32 = jnp.float32
BF16 = jnp.bfloat16
I32 = jnp.int32
HIGH = lax.Precision.HIGHEST
VMEM = pltpu.VMEM
SMEM = pltpu.SMEM
MIB = 1 << 20
CLASSES = ((32, 4), (64, 3), (96, 2), (128, 2))


def harmonics(coord_x, coord_y, coord_z):
    radius_sq = coord_x * coord_x + coord_y * coord_y + coord_z * coord_z
    real_part = {(0, 0): jnp.ones_like(coord_x)}
    imag_part = {}
    for degree in range(1, ORDER):
        scale = 1.0 / (2.0 * degree)
        if degree == 1:
            real_part[1, 1] = coord_x * scale
            imag_part[1, 1] = coord_y * scale
        else:
            prior_re = real_part[degree - 1, degree - 1]
            prior_im = imag_part[degree - 1, degree - 1]
            real_part[degree, degree] = (coord_x * prior_re - coord_y * prior_im) * scale
            imag_part[degree, degree] = (coord_x * prior_im + coord_y * prior_re) * scale
        for column in range(degree):
            factor = 1.0 / ((degree + column) * (degree - column))
            lead = ((2.0 * degree - 1.0) * factor) * coord_z
            for part in (real_part, imag_part):
                if (degree - 1, column) not in part:
                    continue
                value = lead * part[degree - 1, column]
                if column <= degree - 2:
                    value = value - (radius_sq * factor) * part[degree - 2, column]
                part[degree, column] = value
    pieces = []
    for degree in range(ORDER):
        for column in range(degree + 1):
            weight = math.sqrt(math.factorial(degree - column) * math.factorial(degree + column))
            pieces.append(weight * real_part[degree, column])
            if column > 0:
                pieces.append(weight * imag_part[degree, column])
    return pieces


def near_offsets():
    shifts = []
    for step_x in (-1, 0, 1):
        for step_y in (-1, 0, 1):
            for step_z in (-1, 0, 1):
                if step_x != 0 or step_y != 0 or step_z != 0:
                    shifts.append((step_x, step_y, step_z))
    return shifts


def far_groups():
    offsets = []
    for step_x in range(-3, 4):
        for step_y in range(-3, 4):
            for step_z in range(-3, 4):
                if max(abs(step_x), abs(step_y), abs(step_z)) >= 2:
                    offsets.append((step_x, step_y, step_z))
    groups = {}
    for j, offset in enumerate(offsets):
        mask, value = 0, 0
        for axis in range(3):
            if abs(offset[axis]) == 3:
                mask |= 1 << axis
                if offset[axis] == -3:
                    value |= 1 << axis
        key = tuple(abs(v) if abs(v) == 3 else v for v in offset)
        groups.setdefault(key, []).append((j, mask, value))
    return sorted(groups.values(), key=len)


GROUPS = far_groups()


def split3(value):
    high = value.astype(BF16).astype(F32)
    rest = value - high
    mid = rest.astype(BF16).astype(F32)
    return high, mid, rest - mid


def iota(shape, dim):
    return lax.broadcasted_iota(I32, shape, dim)


def pack_kernel(send, part, cnt, tab, out):
    filled = jnp.where(iota((SLOTS, LEAVES), 0) < cnt[...], 1.0, 0.0).T
    comps = [part[0], part[1], part[2], jnp.where(filled > 0.5, part[3], 0.0)]
    for a in range(4):
        tab[pl.ds(a, LEAVES, stride=8), :] = comps[a]
        tab[pl.ds(a + 4, LEAVES, stride=8), :] = comps[a]
    upper = iota((8, 128), 0) < 4

    def body(r, carry):
        for k in range(4):
            first = jnp.maximum(send[r, 2 * k], 0)
            second = jnp.maximum(send[r, 2 * k + 1], 0)
            tile0 = tab[pl.ds(pl.multiple_of(first * 8, 8), 8), :]
            tile1 = tab[pl.ds(pl.multiple_of(second * 8, 8), 8), :]
            out[r, 8 * k : 8 * k + 8, :] = jnp.where(upper, tile0, tile1)
        return carry

    lax.fori_loop(0, RANKS, body, 0, unroll=4)


def pack_near(near_rows, particles, cnt):
    return pl.pallas_call(
        pack_kernel,
        out_shape=(
            jax.ShapeDtypeStruct((LEAVES * 8, 128), F32),
            jax.ShapeDtypeStruct((RANKS, 32, 128), F32),
        ),
        in_specs=[pl.BlockSpec(memory_space=SMEM), pl.BlockSpec(memory_space=VMEM), pl.BlockSpec(memory_space=VMEM)],
        out_specs=(pl.BlockSpec(memory_space=VMEM), pl.BlockSpec(memory_space=VMEM)),
        compiler_params=pltpu.CompilerParams(vmem_limit_bytes=32 * MIB),
        cost_estimate=pl.CostEstimate(flops=3_000_000, bytes_accessed=3 * MIB, transcendentals=0),
        name="pack_near",
    )(near_rows, particles, cnt)


def nt(left, right):
    return lax.dot_general(left, right, (((1,), (1,)), ((), ())), precision=HIGH, preferred_element_type=F32)


def moments_kernel(part, cnt, idx3, tops, upward, sent, leaf_out, mid_out, xs, table):
    filled = iota((SLOTS, LEAVES), 0) < cnt[...]
    for a in range(3):
        xs[a] = part[a].T
    xs[3] = jnp.where(filled, part[3].T, 0.0)

    def chunk(c, acc):
        rows = pl.ds(pl.multiple_of(c * 8, 8), 8)
        charge = xs[3, rows, :]
        basis = harmonics(xs[0, rows, :], xs[1, rows, :], xs[2, rows, :])
        return tuple(old + charge * value for old, value in zip(acc, basis))

    zero = jnp.zeros((8, 128), F32)
    acc = lax.fori_loop(0, SLOTS // 8, chunk, (zero,) * TERMS)
    rows = [jnp.sum(value, axis=0, keepdims=True) for value in acc]
    leaf = jnp.concatenate(rows + [jnp.zeros((4, 128), F32)], axis=0)
    leaf_out[...] = leaf
    table[...] = jnp.zeros((256, 128), F32)
    table[0:128, :] = jnp.concatenate([leaf, jnp.zeros((88, 128), F32)], axis=0).T
    mid = jnp.zeros((16, TERMS), F32)
    for o in range(8):
        mid = mid + nt(table[pl.ds(o, 16, stride=8), :][:, :TERMS], upward[o])
    table[128:144, 0:TERMS] = mid
    top = jnp.zeros((2, TERMS), F32)
    for o in range(8):
        top = top + nt(table[pl.ds(128 + o, 2, stride=8), :][:, :TERMS], upward[o])
    table[144:146, 0:TERMS] = top
    table[160:168, :] = tops[...]
    mid_wide = jnp.concatenate([table[128:144, :], jnp.zeros((112, 128), F32)], axis=0)
    mid_out[...] = mid_wide.T[0:40]
    weights = []
    for a in range(3):
        values = table[...] if a == 0 else pltpu.roll(table[...], 40 * a, 1)
        high, middle, low = split3(values)
        weights.append((jnp.concatenate([high, middle], axis=1).astype(BF16), low.astype(BF16)))
    lane = iota((128, 256), 1)

    def pick(e, carry):
        rows = pl.ds(pl.multiple_of(e * 128, 128), 128)
        columns = idx3[rows, :]
        total = jnp.zeros((128, 128), F32)
        for a in range(3):
            hot = jnp.where(columns[:, a : a + 1] == lane, 1.0, 0.0).astype(BF16)
            both = jnp.dot(hot, weights[a][0], preferred_element_type=F32)
            total = total + (both[:, :128] + both[:, 128:]) + jnp.dot(hot, weights[a][1], preferred_element_type=F32)
        sent[rows, :] = total
        return carry

    lax.fori_loop(0, 8, pick, 0)


def moments(particles, cnt, idx3, tops, upward):
    return pl.pallas_call(
        moments_kernel,
        out_shape=(
            jax.ShapeDtypeStruct((RANKS * 8, 128), F32),
            jax.ShapeDtypeStruct((40, 128), F32),
            jax.ShapeDtypeStruct((40, 128), F32),
        ),
        in_specs=[pl.BlockSpec(memory_space=VMEM)] * 5,
        out_specs=(pl.BlockSpec(memory_space=VMEM),) * 3,
        scratch_shapes=[VMEM((4, SLOTS, LEAVES), F32), VMEM((256, 128), F32)],
        compiler_params=pltpu.CompilerParams(vmem_limit_bytes=32 * MIB),
        cost_estimate=pl.CostEstimate(flops=5_000_000, bytes_accessed=2 * MIB, transcendentals=0),
        name="moments",
    )(particles, cnt, idx3, tops, upward)


def shift_tables():
    scale = np.zeros((32, 8, 128), np.float32)
    add = np.zeros((32, 8, 128), np.float32)
    shifts = near_offsets() + [(0, 0, 0)] * 6
    for j, shift in enumerate(shifts):
        for a in range(3):
            scale[j, a] = 1.0
            scale[j, a + 4] = 1.0
            add[j, a] = 2.0 * shift[a]
            add[j, a + 4] = 2.0 * shift[a]
        add[j, 3] = 1.0
    return scale.reshape(256, 128)[:8], add.reshape(256, 128)


def source_matrix(tile, scale, add, upper):
    moved = tile * scale + add
    values = jnp.where(upper, moved, moved * moved)
    high, middle, low = split3(values)
    return jnp.concatenate([high, high, middle, high, middle, low], axis=0).astype(BF16)


def target_kernel(tab, target):
    upper = iota((8, 128), 0)

    def build(i, carry):
        for l in range(8):
            b = i * 8 + l
            tile = tab[pl.ds(pl.multiple_of(b * 8, 8), 8), :]
            square = jnp.where(upper < 3, tile * tile, 0.0)
            norm = jnp.sum(square, axis=0, keepdims=True) + SOFTEN
            values = jnp.where(upper < 3, -2.0 * tile, jnp.where(upper == 3, norm, jnp.where(upper < 7, 1.0, 0.0)))
            high, middle, low = split3(values)
            wide = jnp.concatenate([high, middle, high, low, middle, high], axis=0)
            target[pl.ds(pl.multiple_of(b * 128, 128), 128), :] = wide.T.astype(BF16)
        return carry

    lax.fori_loop(0, LEAVES // 8, build, 0)


def near_targets(tab):
    return pl.pallas_call(
        target_kernel,
        out_shape=jax.ShapeDtypeStruct((LEAVES * 128, 48), BF16),
        in_specs=[pl.BlockSpec(memory_space=VMEM)],
        out_specs=pl.BlockSpec(memory_space=VMEM),
        compiler_params=pltpu.CompilerParams(vmem_limit_bytes=32 * MIB),
        cost_estimate=pl.CostEstimate(flops=3_000_000_000, bytes_accessed=5 * MIB, transcendentals=0),
        name="near_targets",
    )(tab)


def near_kernel(lists, counts, own, received, scale_in, add_in, target, cnt, far, out, field, tab, order):
    upper = iota((8, 128), 0) < 4
    scale = scale_in[...]
    tab[0 : 8 * LEAVES, :] = own[...]

    def build(s, carry):
        for k in range(4):
            tile = received[s, 8 * k : 8 * k + 8, :]
            turned = pltpu.roll(tile, 4, 0)
            base = pl.multiple_of(8 * LEAVES + s * 64 + k * 16, 16)
            tab[pl.ds(base, 8), :] = jnp.where(upper, tile, turned)
            tab[pl.ds(base + 8, 8), :] = jnp.where(upper, turned, tile)
        return carry

    lax.fori_loop(0, RANKS, build, 0, unroll=4)
    field[...] = far[...]

    def source(place, slot):
        tile = tab[pl.ds(place, 8), :]
        return source_matrix(tile, scale, add_in[slot * 8 : slot * 8 + 8, :], upper), tile[3:4]

    def leaf_field(word, rows):
        b = jnp.minimum(word, LEAVES - 1)
        left = target[pl.ds(pl.multiple_of(b * 128, 128), rows), :]
        total = None
        for pair in range(13):
            picked = [source(pl.multiple_of(lists[2 * pair + l, b] * 8, 8), 2 * pair + l) for l in range(2)]
            square = jnp.dot(left, jnp.concatenate([picked[0][0], picked[1][0]], axis=1), preferred_element_type=F32)
            term = lax.rsqrt(square[:, :128]) * picked[0][1] + lax.rsqrt(square[:, 128:]) * picked[1][1]
            total = term if total is None else total + term
        mat, charge = source(pl.multiple_of(b * 8, 8), 31)
        square = jnp.dot(left, mat, preferred_element_type=F32)
        same = iota((rows, 128), 0) == iota((rows, 128), 1)
        total = total + jnp.where(same, 0.0, lax.rsqrt(square) * charge)
        value = jnp.sum(total, axis=1, keepdims=True)
        field[0:rows, :] = jnp.where(iota((rows, 128), 1) == word, field[0:rows, :] + value, field[0:rows, :])

    base = jnp.int32(0)
    for rows, together in CLASSES:

        def collect(b, count, rows=rows, base=base):
            order[base + count] = b
            inside = (counts[b] <= rows) & (counts[b] > rows - CLASSES[0][0])
            return count + jnp.where(inside, 1, 0)

        count = lax.fori_loop(0, LEAVES, collect, jnp.int32(0))
        for n in range(together):
            order[base + count + n] = LEAVES

        def work(i, carry, rows=rows, together=together, base=base):
            for n in range(together):
                leaf_field(order[base + i * together + n], rows)
            return carry

        lax.fori_loop(0, (count + (together - 1)) // together, work, 0)
        base = base + count

    out[...] = jnp.where(iota((SLOTS, LEAVES), 0) < cnt[...], field[...], 0.0).T


def near_pass(lists, counts, own, received, target, cnt, far):
    scale, add = shift_tables()
    v = pl.BlockSpec(memory_space=VMEM)
    s = pl.BlockSpec(memory_space=SMEM)
    return pl.pallas_call(
        near_kernel,
        out_shape=jax.ShapeDtypeStruct((LEAVES, SLOTS), F32),
        in_specs=[s, s] + [v] * 7,
        out_specs=v,
        scratch_shapes=[VMEM((128, 128), F32), VMEM((8 * (LEAVES + RANKS * 8), 128), F32), SMEM((160,), I32)],
        compiler_params=pltpu.CompilerParams(vmem_limit_bytes=48 * MIB),
        cost_estimate=pl.CostEstimate(flops=30_000_000_000, bytes_accessed=8 * MIB, transcendentals=20_000_000),
        name="near_pass",
    )(lists, counts, own, received, jnp.asarray(scale), jnp.asarray(add), target, cnt, far)


N1 = sum(len(g) == 1 for g in GROUPS)
N2 = sum(len(g) == 2 for g in GROUPS)
N4 = sum(len(g) == 4 for g in GROUPS)
N8 = sum(len(g) == 8 for g in GROUPS)
MERGED = len(GROUPS)
MERGED_PAD = 192


def group_words():
    words = np.zeros((MERGED_PAD, 8), np.int32)
    for m, group in enumerate(GROUPS):
        for g in range(8):
            j, mask, value = group[min(g, len(group) - 1)]
            words[m, g] = j * 64 + mask * 8 + value
    return words


def far_kernel(
    words, where_am_i, recv, leaf, mid, far_lists, small_lists, operators, downward, part,
    out, rt, merged, wide, small, xs, parents, leaves, swapped,
):
    for i in range(8):
        rt[:, 128 * i : 128 * i + 128] = recv[128 * i : 128 * i + 128, :].T

    def two(value):
        high = value.astype(BF16).astype(F32)
        return jnp.concatenate([high, value - high], axis=0).astype(BF16)

    table = two(jnp.concatenate([leaf[...], rt[0:40, :], rt[40:80, :]], axis=1))
    for m, group in enumerate(GROUPS):
        row = far_lists[group[0][0] : group[0][0] + 1, :]
        for j, _, _ in group[1:]:
            row = jnp.maximum(row, far_lists[j : j + 1, :])
        merged[m : m + 1, :] = row
    merged[MERGED:, :] = jnp.full((MERGED_PAD - MERGED, 128), -1, I32)
    index = merged[...]
    rel = index - LEAVES
    slot = rel & 15
    moved = LEAVES + lax.shift_right_logical(slot, 3) * 1024 + lax.shift_right_logical(rel, 4) * 8 + (slot & 7)
    merged[...] = jnp.where(rel >= 0, moved, index)
    lane = iota((40, 128), 1)

    numbers = iota((256, 384), 0).astype(F32).astype(BF16)
    one = jnp.ones((), BF16)
    zero = jnp.zeros((), BF16)

    def hot(row, depth):
        width = row.shape[1]
        upper = lax.shift_right_arithmetic(row, 8)
        lower = (row & 255).astype(F32)
        pieces = []
        for c in range((depth + 255) // 256):
            height = min(256, depth - 256 * c)
            target = jnp.broadcast_to(jnp.where(upper == c, lower, -1.0).astype(BF16), (height, width))
            number = numbers[0:height, 0:width]
            pieces.append(jnp.where(target == number, one, zero))
        return jnp.concatenate(pieces, axis=0)

    def expand(values, m, size):
        for g in range(size):
            word = words[m, g]
            j = lax.shift_right_logical(word, 6)
            keep = (lane & (lax.shift_right_logical(word, 3) & 7)) == (word & 7)
            wide[pl.ds(j, 40, stride=320), :] = jnp.where(keep, values, 0.0)

    def block(first_row, size, together):
        def body(i, carry):
            values = []
            for n in range(together):
                m = first_row + 2 * (together * i + n)
                row = jnp.concatenate([merged[pl.ds(m, 1), :], merged[pl.ds(m + 1, 1), :]], axis=1)
                both = jnp.dot(table, hot(row, 2176), preferred_element_type=F32)
                values.append((m, both[0:40] + both[40:80]))
            for m, value in values:
                expand(value[:, :128], m, size)
                expand(value[:, 128:], m + 1, size)
            return carry

        return body

    lax.fori_loop(0, 7, block(0, 1, 7), 0)
    lax.fori_loop(0, 10, block(N1, 2, 4), 0)
    lax.fori_loop(0, 4, block(N1 + N2, 8, 2), 0)

    def contract(left, right, dims):
        lh = left.astype(BF16)
        ll = (left - lh.astype(F32)).astype(BF16)
        rh = right.astype(BF16)
        rl = (right - rh.astype(F32)).astype(BF16)
        dot = lambda a, b: lax.dot_general(a, b, (dims, ((), ())), preferred_element_type=F32)
        return dot(lh, rh) + dot(ll, rh) + dot(lh, rl)

    for level in range(3):
        swapped[level] = pltpu.einshape("ikj->kij", operators[level])
    local = jnp.zeros((TERMS, 128), F32)
    for k in range(TERMS):
        local = local + contract(swapped[0, k], wide[320 * k : 320 * k + OFFS, :], ((1,), (0,)))

    table_small = two(jnp.concatenate([mid[...], rt[80:120, :]], axis=1))
    lists = small_lists[...]
    rel = lists - 16
    mid_place = jnp.where(rel >= 0, LEAVES + lax.shift_right_logical(rel, 2) * 8 + (rel & 3), lists)
    me = where_am_i[0]
    group = lax.shift_right_logical(me, 5)
    top_place = jnp.where(lists >= 0, LEAVES + (group * 32 + lax.shift_right_arithmetic(lists, 1)) * 8 + 4 + (lists & 1), -1)
    for h in range(4):
        row = recv[pl.ds((h * 32 + (me & 31)) * 8 + 6, 1), :]
        for c in range(4):
            box = row[:, 120 + c : 121 + c].astype(I32)
            place = LEAVES + (h * 32 + lax.shift_right_arithmetic(box, 1)) * 8 + 4 + (box & 1)
            top_place = jnp.where(lists == 64 + 4 * h + c, place, top_place)
    place = jnp.where(iota(lists.shape, 0) < 16, mid_place, top_place)
    for t in range(18):
        both = jnp.dot(table_small, hot(place[t : t + 1], 1152), preferred_element_type=F32)
        value = both[0:40] + both[40:80]
        for c in range(3):
            small[c, 40 * t : 40 * t + 40, :] = value[:, 128 * c : 128 * c + 128]
    mid_local = jnp.zeros((16, TERMS), F32)
    top_local = jnp.zeros((2, TERMS), F32)

    def every_40th(start, size):
        return jnp.concatenate([small[c, pl.ds(start, size, stride=40), :] for c in range(3)], axis=1)[:, :OFFS]

    for k in range(TERMS):
        dims = ((1,), (1,))
        mid_local = mid_local + contract(every_40th(k, 16), swapped[1, k], dims)
        top_local = top_local + contract(every_40th(640 + k, 2), swapped[2, k], dims)

    for o in range(8):
        parents[pl.ds(o, 2, stride=8), 0:TERMS] = nt(top_local, downward[o])
    mid_total = parents[:, 0:TERMS] + mid_local
    leaves[...] = jnp.zeros((128, 128), F32)
    for o in range(8):
        leaves[pl.ds(o, 16, stride=8), 0:TERMS] = nt(mid_total, downward[o])
    leaves[...] = leaves[...].T
    leaves[0:TERMS, :] = leaves[0:TERMS, :] + local
    for a in range(3):
        xs[a] = part[a].T

    def chunk(c, carry):
        rows = pl.ds(pl.multiple_of(c * 8, 8), 8)
        basis = harmonics(xs[0, rows, :], xs[1, rows, :], xs[2, rows, :])
        total = leaves[0:1, :] * basis[0]
        for k in range(1, TERMS):
            total = total + leaves[k : k + 1, :] * basis[k]
        out[rows, :] = total
        return carry

    lax.fori_loop(0, SLOTS // 8, chunk, 0)


def far_pass(where_am_i, recv, leaf, mid, far_lists, small_lists, translate, downward, particles):
    v = pl.BlockSpec(memory_space=VMEM)
    s = pl.BlockSpec(memory_space=SMEM)
    return pl.pallas_call(
        far_kernel,
        out_shape=jax.ShapeDtypeStruct((SLOTS, LEAVES), F32),
        in_specs=[s, s] + [v] * 8,
        out_specs=v,
        scratch_shapes=[
            VMEM((128, 1024), F32),
            VMEM((MERGED_PAD, 128), I32),
            VMEM((40 * 320, 128), F32),
            VMEM((3, 18 * 40, 128), F32),
            VMEM((3, 128, 128), F32),
            VMEM((16, 128), F32),
            VMEM((128, 128), F32),
            VMEM((3, TERMS, TERMS, OFFS), F32),
        ],
        compiler_params=pltpu.CompilerParams(vmem_limit_bytes=48 * MIB),
        cost_estimate=pl.CostEstimate(flops=20_000_000_000, bytes_accessed=10 * MIB, transcendentals=0),
        name="far_pass",
    )(jnp.asarray(group_words()), where_am_i, recv, leaf, mid, far_lists, small_lists, translate, downward, particles)


def local(
    particles,
    counts,
    upward,
    downward,
    translate,
    far_send,
    mid_send,
    top_send,
    near_send,
    far_lists,
    mid_lists,
    top_lists,
    near_lists,
):
    me = lax.axis_index("group") * 32 + lax.axis_index("dev")
    cnt = counts.reshape(1, LEAVES)
    far_rows = far_send[0]
    mid_rows = jnp.where(mid_send[0] >= 0, mid_send[0] + 128, -1)
    rank = jnp.arange(RANKS, dtype=I32)[:, None]
    tail = jnp.concatenate([jnp.full((RANKS, 1), 144, I32), jnp.full((RANKS, 1), 145, I32), 160 + rank // 32, jnp.full((RANKS, 1), -1, I32)], axis=1)
    idx3 = jnp.stack([far_rows[:, :8], far_rows[:, 8:], jnp.concatenate([mid_rows, tail], axis=1)], axis=-1)
    tops = jnp.pad(top_send[0].astype(F32), ((0, 4), (40, 84)))
    sent, leaf, mid = moments(particles, cnt, idx3.reshape(RANKS * 8, 3), tops, upward)
    recv = lax.all_to_all(sent.reshape(RANKS, 8, 128), AXES, split_axis=0, concat_axis=0, tiled=True)

    tab, near_out = pack_near(near_send[0], particles, cnt)
    target = near_targets(tab)
    small_lists = jnp.pad(jnp.concatenate([mid_lists, top_lists], axis=1).T, ((0, 6), (0, 68)), constant_values=-1)
    near_out, recv, target, small_lists = lax.optimization_barrier((near_out, recv, target, small_lists))
    near_in = lax.all_to_all(near_out, AXES, split_axis=0, concat_axis=0, tiled=True)
    far = far_pass(me.reshape(1), recv.reshape(RANKS * 8, 128), leaf, mid, far_lists, small_lists, translate, downward, particles)
    return near_pass(near_lists, counts, tab, near_in, target, cnt, far)


def solution(mesh):
    in_specs = (
        P(None, AXES, None),
        P(AXES),
        P(),
        P(),
        P(),
        P(AXES, None, None),
        P(AXES, None, None),
        P(AXES, None, None),
        P(AXES, None, None),
        P(None, AXES),
        P(None, AXES),
        P(None, AXES),
        P(None, AXES),
    )
    return jax.shard_map(local, mesh=mesh, in_specs=in_specs, out_specs=P(AXES, None), check_vma=False)
```

```python
import math

import jax
import jax.numpy as jnp
import numpy as np
from jax import lax
from jax.experimental import pallas as pl
from jax.experimental.pallas import tpu as pltpu
from jax.sharding import PartitionSpec as P

ORDER = 6
TERMS = 36
OFFS = 316
SOFTEN = 0.01
LEAVES = 128
SLOTS = 128
RANKS = 128
AXES = ("group", "dev")
F32 = jnp.float32
BF16 = jnp.bfloat16
I32 = jnp.int32
HIGH = lax.Precision.HIGHEST
VMEM = pltpu.VMEM
SMEM = pltpu.SMEM
MIB = 1 << 20
OWN_SLOTS = 17
REST_SLOTS = 10
DUMMY = LEAVES
OWN_CLASSES = (8, 6, 4, 4)
REST_CLASSES = (11, 8, 8, 8)


def harmonics(coord_x, coord_y, coord_z):
    radius_sq = coord_x * coord_x + coord_y * coord_y + coord_z * coord_z
    real_part = {(0, 0): jnp.ones_like(coord_x)}
    imag_part = {}
    for degree in range(1, ORDER):
        scale = 1.0 / (2.0 * degree)
        if degree == 1:
            real_part[1, 1] = coord_x * scale
            imag_part[1, 1] = coord_y * scale
        else:
            prior_re = real_part[degree - 1, degree - 1]
            prior_im = imag_part[degree - 1, degree - 1]
            real_part[degree, degree] = (coord_x * prior_re - coord_y * prior_im) * scale
            imag_part[degree, degree] = (coord_x * prior_im + coord_y * prior_re) * scale
        for column in range(degree):
            factor = 1.0 / ((degree + column) * (degree - column))
            lead = ((2.0 * degree - 1.0) * factor) * coord_z
            for part in (real_part, imag_part):
                if (degree - 1, column) not in part:
                    continue
                value = lead * part[degree - 1, column]
                if column <= degree - 2:
                    value = value - (radius_sq * factor) * part[degree - 2, column]
                part[degree, column] = value
    pieces = []
    for degree in range(ORDER):
        for column in range(degree + 1):
            weight = math.sqrt(math.factorial(degree - column) * math.factorial(degree + column))
            pieces.append(weight * real_part[degree, column])
            if column > 0:
                pieces.append(weight * imag_part[degree, column])
    return pieces


def near_offsets():
    shifts = []
    for step_x in (-1, 0, 1):
        for step_y in (-1, 0, 1):
            for step_z in (-1, 0, 1):
                if step_x != 0 or step_y != 0 or step_z != 0:
                    shifts.append((step_x, step_y, step_z))
    return shifts


def far_groups():
    offsets = []
    for step_x in range(-3, 4):
        for step_y in range(-3, 4):
            for step_z in range(-3, 4):
                if max(abs(step_x), abs(step_y), abs(step_z)) >= 2:
                    offsets.append((step_x, step_y, step_z))
    groups = {}
    for j, offset in enumerate(offsets):
        mask, value = 0, 0
        for axis in range(3):
            if abs(offset[axis]) == 3:
                mask |= 1 << axis
                if offset[axis] == -3:
                    value |= 1 << axis
        key = tuple(abs(v) if abs(v) == 3 else v for v in offset)
        groups.setdefault(key, []).append((j, mask, value))
    return sorted(groups.values(), key=len)


GROUPS = far_groups()


def split3(value):
    high = value.astype(BF16).astype(F32)
    rest = value - high
    mid = rest.astype(BF16).astype(F32)
    return high, mid, rest - mid


def iota(shape, dim):
    return lax.broadcasted_iota(I32, shape, dim)


def nt(left, right):
    return lax.dot_general(left, right, (((1,), (1,)), ((), ())), precision=HIGH, preferred_element_type=F32)


def send_kernel(near_send, part, cnt, far_send, mid_send, tops, upward, sent, tab, leaf_out, mid_out, xs, table):
    filled = iota((SLOTS, LEAVES), 0) < cnt[...]
    for a in range(3):
        xs[a] = part[a].T
    xs[3] = jnp.where(filled, part[3].T, 0.0)
    comps = [part[0], part[1], part[2], xs[3].T]
    for a in range(4):
        tab[pl.ds(a, LEAVES, stride=8), :] = comps[a]
        tab[pl.ds(a + 4, LEAVES, stride=8), :] = comps[a]
    tab[8 * DUMMY : 8 * DUMMY + 8, :] = jnp.zeros((8, 128), F32)
    upper = iota((8, 128), 0) < 4

    def pack(i, carry):
        for n in range(4):
            r = i * 4 + n
            for k in range(4):
                first = jnp.maximum(near_send[r, 2 * k], 0)
                second = jnp.maximum(near_send[r, 2 * k + 1], 0)
                tile0 = tab[pl.ds(pl.multiple_of(first * 8, 8), 8), :]
                tile1 = tab[pl.ds(pl.multiple_of(second * 8, 8), 8), :]
                sent[r, 8 * k : 8 * k + 8, :] = jnp.where(upper, tile0, tile1)
        return carry

    lax.fori_loop(0, RANKS // 4, pack, 0)

    def chunk(c, acc):
        rows = pl.ds(pl.multiple_of(c * 16, 16), 16)
        charge = xs[3, rows, :]
        basis = harmonics(xs[0, rows, :], xs[1, rows, :], xs[2, rows, :])
        terms = [charge * value for value in basis]
        return tuple(old + (term[0:8] + term[8:16]) for old, term in zip(acc, terms))

    zero = jnp.zeros((8, 128), F32)
    acc = lax.fori_loop(0, SLOTS // 16, chunk, (zero,) * TERMS)
    rows = [jnp.sum(value, axis=0, keepdims=True) for value in acc]
    leaf = jnp.concatenate(rows + [jnp.zeros((4, 128), F32)], axis=0)
    leaf_out[...] = leaf
    table[...] = jnp.zeros((256, 128), F32)
    table[0:128, :] = jnp.concatenate([leaf, jnp.zeros((88, 128), F32)], axis=0).T
    mid = jnp.zeros((16, TERMS), F32)
    for o in range(8):
        mid = mid + nt(table[pl.ds(o, 16, stride=8), :][:, :TERMS], upward[o])
    table[128:144, 0:TERMS] = mid
    top = jnp.zeros((2, TERMS), F32)
    for o in range(8):
        top = top + nt(table[pl.ds(128 + o, 2, stride=8), :][:, :TERMS], upward[o])
    table[144:146, 0:TERMS] = top
    table[160:168, :] = tops[...]
    mid_wide = jnp.concatenate([table[128:144, :], jnp.zeros((112, 128), F32)], axis=0)
    mid_out[...] = mid_wide.T[0:40]
    weights = []
    for a in range(3):
        values = table[...] if a == 0 else pltpu.roll(table[...], 40 * a, 1)
        high, middle, low = split3(values)
        weights.append((jnp.concatenate([high, middle], axis=1).astype(BF16), low.astype(BF16)))
    lane = iota((128, 256), 1)

    def chosen(a, column):
        hot = jnp.where(column == lane, 1.0, 0.0).astype(BF16)
        both = jnp.dot(hot, weights[a][0], preferred_element_type=F32)
        return both[:, :128] + both[:, 128:] + jnp.dot(hot, weights[a][1], preferred_element_type=F32)

    for c in range(8):
        total = chosen(0, far_send[:, c : c + 1]) + chosen(1, far_send[:, c + 8 : c + 9])
        if c < 4:
            column = mid_send[:, c : c + 1]
            total = total + chosen(2, jnp.where(column >= 0, column + 128, -1))
        elif c < 6:
            total = total + pltpu.roll(table[140 + c : 141 + c, :], 80, 1)
        elif c == 6:
            group = lax.shift_right_logical(iota((RANKS, 128), 0), 5)
            for g in range(4):
                total = total + jnp.where(group == g, pltpu.roll(table[160 + g : 161 + g, :], 80, 1), 0.0)
        sent[:, 32 + c, :] = total


def send_pass(near_send, particles, cnt, far_send, mid_send, tops, upward):
    return pl.pallas_call(
        send_kernel,
        out_shape=(
            jax.ShapeDtypeStruct((RANKS, 40, 128), F32),
            jax.ShapeDtypeStruct(((LEAVES + 1) * 8, 128), F32),
            jax.ShapeDtypeStruct((40, 128), F32),
            jax.ShapeDtypeStruct((40, 128), F32),
        ),
        in_specs=[pl.BlockSpec(memory_space=SMEM)] + [pl.BlockSpec(memory_space=VMEM)] * 6,
        out_specs=(pl.BlockSpec(memory_space=VMEM),) * 4,
        scratch_shapes=[VMEM((4, SLOTS, LEAVES), F32), VMEM((256, 128), F32)],
        compiler_params=pltpu.CompilerParams(vmem_limit_bytes=32 * MIB),
        cost_estimate=pl.CostEstimate(flops=5_000_000, bytes_accessed=2 * MIB, transcendentals=0),
        name="send_pass",
    )(near_send, particles, cnt, far_send, mid_send, tops, upward)


def shift_tables():
    scale = np.zeros((32, 8, 128), np.float32)
    add = np.zeros((32, 8, 128), np.float32)
    shifts = near_offsets() + [(0, 0, 0)] * 6
    for j, shift in enumerate(shifts):
        for a in range(3):
            scale[j, a] = 1.0
            scale[j, a + 4] = 1.0
            add[j, a] = 2.0 * shift[a]
            add[j, a + 4] = 2.0 * shift[a]
        add[j, 3] = 1.0
    return scale.reshape(256, 128)[:8], add.reshape(256, 128)


def source_matrix(tile, scale, add, upper):
    moved = tile * scale + add
    values = jnp.where(upper, moved, moved * moved)
    high, middle, low = split3(values)
    return jnp.concatenate([high, high, middle, high, middle, low], axis=0).astype(BF16)


def build_targets(tab, target):
    upper = iota((8, 128), 0)

    def build(i, carry):
        for l in range(8):
            b = i * 8 + l
            tile = tab[pl.ds(pl.multiple_of(b * 8, 8), 8), :]
            square = jnp.where(upper < 3, tile * tile, 0.0)
            norm = jnp.sum(square, axis=0, keepdims=True) + SOFTEN
            values = jnp.where(upper < 3, -2.0 * tile, jnp.where(upper == 3, norm, jnp.where(upper < 7, 1.0, 0.0)))
            high, middle, low = split3(values)
            wide = jnp.concatenate([high, middle, high, low, middle, high], axis=0)
            target[pl.ds(pl.multiple_of(b * 128, 128), 128), :] = wide.T.astype(BF16)
        return carry

    lax.fori_loop(0, LEAVES // 8, build, 0)


def sort_leaves(counts, order, number):
    for k in range(4):
        number[k] = 0

    def collect(i, carry):
        for n in range(8):
            b = i * 8 + n
            k = lax.shift_right_logical(counts[b] - 1, 5)
            place = number[k]
            order[k * 160 + place] = b
            number[k] = place + 1
        return carry

    lax.fori_loop(0, LEAVES // 8, collect, 0)
    for k in range(4):
        for n in range(16):
            order[k * 160 + number[k] + n] = LEAVES


def near_steps(lists, tab, add_in, scale, target, field, order, number, slots, classes, own):
    upper = iota((8, 128), 0) < 4

    def source(place, shift):
        tile = tab[pl.ds(place, 8), :]
        return source_matrix(tile, scale, add_in[pl.ds(shift, 8), :], upper), tile[3:4]

    def listed(m, b):
        word = lists[m, b]
        return source(pl.multiple_of(lax.shift_right_logical(word, 5) * 8, 8), pl.multiple_of((word & 31) * 8, 8))

    def leaf_field(word, rows, start=0):
        b = jnp.minimum(word, LEAVES - 1)
        left = target[pl.ds(pl.multiple_of(b * 128, 128), rows), :]
        picked = [listed(start + m, b) for m in range(slots)]
        if own:
            picked.append(source(pl.multiple_of(b * 8, 8), 31 * 8))
        total = None
        for p in range(0, len(picked), 2):
            (mat0, charge0), (mat1, charge1) = picked[p], picked[p + 1]
            square = jnp.dot(left, jnp.concatenate([mat0, mat1], axis=1), preferred_element_type=F32)
            second = lax.rsqrt(square[:, 128:]) * charge1
            if own and p + 2 == len(picked):
                second = jnp.where(iota((rows, 128), 0) == iota((rows, 128), 1), 0.0, second)
            term = lax.rsqrt(square[:, :128]) * charge0 + second
            total = term if total is None else total + term
        value = jnp.sum(total, axis=1, keepdims=True)
        field[0:rows, :] = jnp.where(iota((rows, 128), 1) == word, field[0:rows, :] + value, field[0:rows, :])

    for k in range(4):
        rows, together = 32 * (k + 1), classes[k]
        def work(i, carry, rows=rows, together=together, k=k):
            for n in range(together):
                leaf_field(order[k * 160 + i * together + n], rows)
            return carry

        lax.fori_loop(0, (number[k] + (together - 1)) // together, work, 0)
    return leaf_field


def near_own_kernel(lists, counts, tab, scale_in, add_in, field, target, order, number):
    field[...] = jnp.zeros((SLOTS, LEAVES), F32)
    build_targets(tab, target)
    sort_leaves(counts, order, number)
    near_steps(lists, tab, add_in, scale_in[...], target, field, order, number, OWN_SLOTS, OWN_CLASSES, True)


def near_rest_kernel(lists, order, number, extra, own, received, scale_in, add_in, target, cnt, near, far, out, field, tab):
    upper = iota((8, 128), 0) < 4
    tab[0 : 8 * (LEAVES + 1), :] = own[...]

    def build(i, carry):
        for n in range(4):
            s = i * 4 + n
            for k in range(4):
                tile = received[s, 8 * k : 8 * k + 8, :]
                turned = pltpu.roll(tile, 4, 0)
                base = pl.multiple_of(8 * (LEAVES + 1) + s * 64 + k * 16, 8)
                tab[pl.ds(base, 8), :] = jnp.where(upper, tile, turned)
                tab[pl.ds(base + 8, 8), :] = jnp.where(upper, turned, tile)
        return carry

    lax.fori_loop(0, RANKS // 4, build, 0)
    field[...] = near[...] + far[...]
    leaf_field = near_steps(lists, tab, add_in, scale_in[...], target, field, order, number, REST_SLOTS, REST_CLASSES, False)

    def more(b, carry):
        def again(c, carry):
            leaf_field(b, SLOTS, c * REST_SLOTS)
            return carry

        return lax.fori_loop(1, extra[b], again, carry)

    lax.fori_loop(0, LEAVES, more, 0)
    out[...] = jnp.where(iota((SLOTS, LEAVES), 0) < cnt[...], field[...], 0.0).T


def near_own(lists, counts, tab):
    scale, add = shift_tables()
    v = pl.BlockSpec(memory_space=VMEM)
    s = pl.BlockSpec(memory_space=SMEM)
    return pl.pallas_call(
        near_own_kernel,
        out_shape=(
            jax.ShapeDtypeStruct((SLOTS, LEAVES), F32),
            jax.ShapeDtypeStruct((LEAVES * 128, 48), BF16),
            jax.ShapeDtypeStruct((640,), I32),
            jax.ShapeDtypeStruct((8,), I32),
        ),
        in_specs=[s, s] + [v] * 3,
        out_specs=(v, v, s, s),
        compiler_params=pltpu.CompilerParams(vmem_limit_bytes=32 * MIB),
        cost_estimate=pl.CostEstimate(flops=30_000_000_000, bytes_accessed=4 * MIB, transcendentals=20_000_000),
        name="near_own",
    )(lists, counts, tab, jnp.asarray(scale), jnp.asarray(add))


def near_rest(lists, order, number, extra, tab, received, target, cnt, near, far):
    scale, add = shift_tables()
    v = pl.BlockSpec(memory_space=VMEM)
    s = pl.BlockSpec(memory_space=SMEM)
    return pl.pallas_call(
        near_rest_kernel,
        out_shape=jax.ShapeDtypeStruct((LEAVES, SLOTS), F32),
        in_specs=[s, s, s, s] + [v] * 8,
        out_specs=v,
        scratch_shapes=[
            VMEM((SLOTS, LEAVES), F32),
            VMEM((8 * (LEAVES + 1 + RANKS * 8), 128), F32),
        ],
        compiler_params=pltpu.CompilerParams(vmem_limit_bytes=48 * MIB),
        cost_estimate=pl.CostEstimate(flops=10_000_000_000, bytes_accessed=8 * MIB, transcendentals=20_000_000),
        name="near_rest",
    )(lists, order, number, extra, tab, received, jnp.asarray(scale), jnp.asarray(add), target, cnt, near, far)


def near_tables(near_lists):
    own = near_lists < LEAVES
    before = jnp.cumsum(own.astype(I32), axis=0)
    slot = jnp.arange(26, dtype=I32)[:, None]
    early = own & (before <= OWN_SLOTS)
    taken = jnp.minimum(before, OWN_SLOTS)
    empty = DUMMY * 32 + 31
    word = jnp.where(own, near_lists, near_lists + 1) * 32 + slot - empty
    tables = []
    for mine, place, size in ((early, before - 1, OWN_SLOTS), (~early, slot - taken, 3 * REST_SLOTS)):
        hits = jnp.where(mine, place, -1)[None] == jnp.arange(size, dtype=I32)[:, None, None]
        tables.append(jnp.sum(jnp.where(hits, word[None], 0), axis=1) + empty)
    goes = (26 - taken[25] + (REST_SLOTS - 1)) // REST_SLOTS
    return tables[0], tables[1], goes


N1 = sum(len(g) == 1 for g in GROUPS)
N2 = sum(len(g) == 2 for g in GROUPS)
N4 = sum(len(g) == 4 for g in GROUPS)
N8 = sum(len(g) == 8 for g in GROUPS)
MERGED = len(GROUPS)
MERGED_PAD = 192


def group_words():
    words = np.zeros((MERGED_PAD, 8), np.int32)
    for m, group in enumerate(GROUPS):
        for g in range(8):
            j, mask, value = group[min(g, len(group) - 1)]
            words[m, g] = j * 64 + mask * 8 + value
    return words


def far_kernel(
    words, where_am_i, recv, leaf, mid, far_lists, small_lists, operators, downward, part,
    out, rt, merged, wide, small, xs, parents, leaves, swapped,
):
    for i in range(8):
        rt[:, 128 * i : 128 * i + 128] = recv[16 * i : 16 * i + 16, 32:40, :].reshape(128, 128).T

    def two(value):
        high = value.astype(BF16).astype(F32)
        return jnp.concatenate([high, value - high], axis=0).astype(BF16)

    table = jnp.concatenate(
        [
            two(jnp.concatenate([leaf[...], rt[0:40, :]], axis=1)),
            two(jnp.concatenate([jnp.zeros((40, 128), F32), rt[40:80, :]], axis=1)),
        ],
        axis=0,
    )
    for m, group in enumerate(GROUPS):
        row = far_lists[group[0][0] : group[0][0] + 1, :]
        for j, _, _ in group[1:]:
            row = jnp.maximum(row, far_lists[j : j + 1, :])
        merged[m : m + 1, :] = row
    merged[MERGED:, :] = jnp.full((MERGED_PAD - MERGED, 128), -1, I32)
    index = merged[...]
    rel = index - LEAVES
    slot = rel & 15
    moved = lax.shift_right_logical(slot, 3) * 8192 + LEAVES + lax.shift_right_logical(rel, 4) * 8 + (slot & 7)
    merged[...] = jnp.where(rel >= 0, moved, index)
    lane = iota((40, 128), 1)

    numbers = iota((256, 384), 0).astype(F32).astype(BF16)
    one = jnp.ones((), BF16)
    zero = jnp.zeros((), BF16)

    def hot(row, depth):
        width = row.shape[1]
        upper = lax.shift_right_arithmetic(row, 8)
        lower = (row & 255).astype(F32)
        pieces = []
        for c in range((depth + 255) // 256):
            height = min(256, depth - 256 * c)
            target = jnp.broadcast_to(jnp.where(upper == c, lower, -1.0).astype(BF16), (height, width))
            number = numbers[0:height, 0:width]
            pieces.append(jnp.where(target == number, one, zero))
        return jnp.concatenate(pieces, axis=0)

    def expand(values, m, size):
        for g in range(size):
            word = words[m, g]
            j = lax.shift_right_logical(word, 6)
            keep = (lane & (lax.shift_right_logical(word, 3) & 7)) == (word & 7)
            wide[pl.ds(j, 40, stride=320), :] = jnp.where(keep, values, 0.0)

    def block(first_row, size, together):
        def body(i, carry):
            values = []
            for n in range(together):
                m = first_row + 2 * (together * i + n)
                row = jnp.concatenate([merged[pl.ds(m, 1), :], merged[pl.ds(m + 1, 1), :]], axis=1)
                late = row >= 8192
                both = jnp.dot(table, hot(jnp.where(late, row - 8192, row), 1152), preferred_element_type=F32)
                values.append((m, jnp.where(late, both[80:120] + both[120:160], both[0:40] + both[40:80])))
            for m, value in values:
                expand(value[:, :128], m, size)
                expand(value[:, 128:], m + 1, size)
            return carry

        return body

    lax.fori_loop(0, 4, block(0, 1, 13), 0)
    lax.fori_loop(0, 4, block(N1, 2, 10), 0)
    lax.fori_loop(0, 2, block(N1 + N2, 8, 4), 0)

    def contract(left, right, dims):
        lh = left.astype(BF16)
        ll = (left - lh.astype(F32)).astype(BF16)
        rh = right.astype(BF16)
        rl = (right - rh.astype(F32)).astype(BF16)
        dot = lambda a, b: lax.dot_general(a, b, (dims, ((), ())), preferred_element_type=F32)
        return dot(lh, rh) + dot(ll, rh) + dot(lh, rl)

    for level in range(3):
        swapped[level] = pltpu.einshape("ikj->kij", operators[level])
    local = jnp.zeros((TERMS, 128), F32)
    for k in range(TERMS):
        local = local + contract(swapped[0, k], wide[320 * k : 320 * k + OFFS, :], ((1,), (0,)))

    table_small = two(jnp.concatenate([mid[...], rt[80:120, :]], axis=1))
    lists = small_lists[...]
    rel = lists - 16
    mid_place = jnp.where(rel >= 0, LEAVES + lax.shift_right_logical(rel, 2) * 8 + (rel & 3), lists)
    me = where_am_i[0]
    group = lax.shift_right_logical(me, 5)
    top_place = jnp.where(lists >= 0, LEAVES + (group * 32 + lax.shift_right_arithmetic(lists, 1)) * 8 + 4 + (lists & 1), -1)
    for h in range(4):
        row = recv[h * 32 + (me & 31), 32:40, :][6:7]
        for c in range(4):
            box = row[:, 120 + c : 121 + c].astype(I32)
            place = LEAVES + (h * 32 + lax.shift_right_arithmetic(box, 1)) * 8 + 4 + (box & 1)
            top_place = jnp.where(lists == 64 + 4 * h + c, place, top_place)
    place = jnp.where(iota(lists.shape, 0) < 16, mid_place, top_place)
    for t in range(18):
        both = jnp.dot(table_small, hot(place[t : t + 1], 1152), preferred_element_type=F32)
        value = both[0:40] + both[40:80]
        for c in range(3):
            small[c, 40 * t : 40 * t + 40, :] = value[:, 128 * c : 128 * c + 128]
    mid_local = jnp.zeros((16, TERMS), F32)
    top_local = jnp.zeros((2, TERMS), F32)

    def every_40th(start, size):
        return jnp.concatenate([small[c, pl.ds(start, size, stride=40), :] for c in range(3)], axis=1)[:, :OFFS]

    for k in range(TERMS):
        dims = ((1,), (1,))
        mid_local = mid_local + contract(every_40th(k, 16), swapped[1, k], dims)
        top_local = top_local + contract(every_40th(640 + k, 2), swapped[2, k], dims)

    for o in range(8):
        parents[pl.ds(o, 2, stride=8), 0:TERMS] = nt(top_local, downward[o])
    mid_total = parents[:, 0:TERMS] + mid_local
    leaves[...] = jnp.zeros((128, 128), F32)
    for o in range(8):
        leaves[pl.ds(o, 16, stride=8), 0:TERMS] = nt(mid_total, downward[o])
    leaves[...] = leaves[...].T
    leaves[0:TERMS, :] = leaves[0:TERMS, :] + local
    for a in range(3):
        xs[a] = part[a].T

    def chunk(c, carry):
        rows = pl.ds(pl.multiple_of(c * 16, 16), 16)
        basis = harmonics(xs[0, rows, :], xs[1, rows, :], xs[2, rows, :])
        total = leaves[0:1, :] * basis[0]
        for k in range(1, TERMS):
            total = total + leaves[k : k + 1, :] * basis[k]
        out[rows, :] = total
        return carry

    lax.fori_loop(0, SLOTS // 16, chunk, 0)


def far_pass(where_am_i, recv, leaf, mid, far_lists, small_lists, translate, downward, particles):
    v = pl.BlockSpec(memory_space=VMEM)
    s = pl.BlockSpec(memory_space=SMEM)
    return pl.pallas_call(
        far_kernel,
        out_shape=jax.ShapeDtypeStruct((SLOTS, LEAVES), F32),
        in_specs=[s, s] + [v] * 8,
        out_specs=v,
        scratch_shapes=[
            VMEM((128, 1024), F32),
            VMEM((MERGED_PAD, 128), I32),
            VMEM((40 * 320, 128), F32),
            VMEM((3, 18 * 40, 128), F32),
            VMEM((3, 128, 128), F32),
            VMEM((16, 128), F32),
            VMEM((128, 128), F32),
            VMEM((3, TERMS, TERMS, OFFS), F32),
        ],
        compiler_params=pltpu.CompilerParams(vmem_limit_bytes=48 * MIB),
        cost_estimate=pl.CostEstimate(flops=20_000_000_000, bytes_accessed=10 * MIB, transcendentals=0),
        name="far_pass",
    )(jnp.asarray(group_words()), where_am_i, recv, leaf, mid, far_lists, small_lists, translate, downward, particles)


def local(
    particles,
    counts,
    upward,
    downward,
    translate,
    far_send,
    mid_send,
    top_send,
    near_send,
    far_lists,
    mid_lists,
    top_lists,
    near_lists,
):
    me = lax.axis_index("group") * 32 + lax.axis_index("dev")
    cnt = counts.reshape(1, LEAVES)
    tops = jnp.pad(top_send[0].astype(F32), ((0, 4), (40, 84)))
    sent, tab, leaf, mid = send_pass(near_send[0], particles, cnt, far_send[0], mid_send[0], tops, upward)
    recv = lax.all_to_all(sent, AXES, split_axis=0, concat_axis=0, tiled=True)

    early, late, goes = near_tables(near_lists)
    small_lists = jnp.pad(jnp.concatenate([mid_lists, top_lists], axis=1).T, ((0, 6), (0, 68)), constant_values=-1)
    near, target, order, number = near_own(early, counts, tab)
    far = far_pass(me.reshape(1), recv, leaf, mid, far_lists, small_lists, translate, downward, particles)
    return near_rest(late, order, number, goes, tab, recv, target, cnt, near, far)


def solution(mesh):
    in_specs = (
        P(None, AXES, None),
        P(AXES),
        P(),
        P(),
        P(),
        P(AXES, None, None),
        P(AXES, None, None),
        P(AXES, None, None),
        P(AXES, None, None),
        P(None, AXES),
        P(None, AXES),
        P(None, AXES),
        P(None, AXES),
    )
    return jax.shard_map(local, mesh=mesh, in_specs=in_specs, out_specs=P(AXES, None), check_vma=False)
```

```python
import math

import jax
import jax.numpy as jnp
import numpy as np
from jax import lax
from jax.experimental import pallas as pl
from jax.experimental.pallas import tpu as pltpu
from jax.sharding import PartitionSpec as P

ORDER = 6
TERMS = 36
OFFS = 316
SOFTEN = 0.01
LEAVES = 128
SLOTS = 128
RANKS = 128
AXES = ("group", "dev")
F32 = jnp.float32
BF16 = jnp.bfloat16
I32 = jnp.int32
HIGH = lax.Precision.HIGHEST
VMEM = pltpu.VMEM
SMEM = pltpu.SMEM
MIB = 1 << 20
OWN_SLOTS = 17
REST_SLOTS = 10
DUMMY = LEAVES
OWN_CLASSES = (11, 8, 6, 6)
REST_CLASSES = (16, 11, 11, 11)


def harmonics(coord_x, coord_y, coord_z):
    radius_sq = coord_x * coord_x + coord_y * coord_y + coord_z * coord_z
    real_part = {(0, 0): jnp.ones_like(coord_x)}
    imag_part = {}
    for degree in range(1, ORDER):
        scale = 1.0 / (2.0 * degree)
        if degree == 1:
            real_part[1, 1] = coord_x * scale
            imag_part[1, 1] = coord_y * scale
        else:
            prior_re = real_part[degree - 1, degree - 1]
            prior_im = imag_part[degree - 1, degree - 1]
            real_part[degree, degree] = (coord_x * prior_re - coord_y * prior_im) * scale
            imag_part[degree, degree] = (coord_x * prior_im + coord_y * prior_re) * scale
        for column in range(degree):
            factor = 1.0 / ((degree + column) * (degree - column))
            lead = ((2.0 * degree - 1.0) * factor) * coord_z
            for part in (real_part, imag_part):
                if (degree - 1, column) not in part:
                    continue
                value = lead * part[degree - 1, column]
                if column <= degree - 2:
                    value = value - (radius_sq * factor) * part[degree - 2, column]
                part[degree, column] = value
    pieces = []
    for degree in range(ORDER):
        for column in range(degree + 1):
            weight = math.sqrt(math.factorial(degree - column) * math.factorial(degree + column))
            pieces.append(weight * real_part[degree, column])
            if column > 0:
                pieces.append(weight * imag_part[degree, column])
    return pieces


def near_offsets():
    shifts = []
    for step_x in (-1, 0, 1):
        for step_y in (-1, 0, 1):
            for step_z in (-1, 0, 1):
                if step_x != 0 or step_y != 0 or step_z != 0:
                    shifts.append((step_x, step_y, step_z))
    return shifts


def far_groups():
    offsets = []
    for step_x in range(-3, 4):
        for step_y in range(-3, 4):
            for step_z in range(-3, 4):
                if max(abs(step_x), abs(step_y), abs(step_z)) >= 2:
                    offsets.append((step_x, step_y, step_z))
    groups = {}
    for j, offset in enumerate(offsets):
        mask, value = 0, 0
        for axis in range(3):
            if abs(offset[axis]) == 3:
                mask |= 1 << axis
                if offset[axis] == -3:
                    value |= 1 << axis
        key = tuple(abs(v) if abs(v) == 3 else v for v in offset)
        groups.setdefault(key, []).append((j, mask, value))
    return sorted(groups.values(), key=len)


GROUPS = far_groups()


def split3(value):
    high = value.astype(BF16).astype(F32)
    rest = value - high
    mid = rest.astype(BF16).astype(F32)
    return high, mid, rest - mid


def iota(shape, dim):
    return lax.broadcasted_iota(I32, shape, dim)


def nt(left, right):
    return lax.dot_general(left, right, (((1,), (1,)), ((), ())), precision=HIGH, preferred_element_type=F32)


def send_kernel(near_send, tops, part, cnt, far_rows, mid_rows, upward_in, sent, tab, leaf_out, mid_out, xs, table):
    filled = iota((SLOTS, LEAVES), 0) < cnt[...]
    for a in range(3):
        xs[a] = part[a].T
    xs[3] = jnp.where(filled, part[3].T, 0.0)
    comps = [part[0], part[1], part[2], xs[3].T]
    for a in range(4):
        tab[pl.ds(a, LEAVES, stride=8), :] = comps[a]
        tab[pl.ds(a + 4, LEAVES, stride=8), :] = comps[a]
    tab[8 * DUMMY : 8 * DUMMY + 8, :] = jnp.zeros((8, 128), F32)
    upper = iota((8, 128), 0) < 4

    def pack(i, carry):
        for n in range(4):
            r = i * 4 + n
            for k in range(4):
                first = jnp.maximum(near_send[2 * k, r], 0)
                second = jnp.maximum(near_send[2 * k + 1, r], 0)
                tile0 = tab[pl.ds(pl.multiple_of(first * 8, 8), 8), :]
                tile1 = tab[pl.ds(pl.multiple_of(second * 8, 8), 8), :]
                sent[r, 8 * k : 8 * k + 8, :] = jnp.where(upper, tile0, tile1)
        return carry

    lax.fori_loop(0, RANKS // 4, pack, 0)

    def chunk(c, acc):
        rows = pl.ds(pl.multiple_of(c * 16, 16), 16)
        charge = xs[3, rows, :]
        basis = harmonics(xs[0, rows, :], xs[1, rows, :], xs[2, rows, :])
        terms = [charge * value for value in basis]
        return tuple(old + (term[0:8] + term[8:16]) for old, term in zip(acc, terms))

    zero = jnp.zeros((8, 128), F32)
    acc = lax.fori_loop(0, SLOTS // 16, chunk, (zero,) * TERMS)
    rows = [jnp.sum(value, axis=0, keepdims=True) for value in acc]
    leaf = jnp.concatenate(rows + [jnp.zeros((4, 128), F32)], axis=0)
    leaf_out[...] = leaf
    table[...] = jnp.zeros((256, 128), F32)
    table[0:128, :] = jnp.concatenate([leaf, jnp.zeros((88, 128), F32)], axis=0).T
    upward = pltpu.einshape("iok->oik", upward_in[...])
    mid = jnp.zeros((16, TERMS), F32)
    for o in range(8):
        mid = mid + nt(table[pl.ds(o, 16, stride=8), :][:, :TERMS], upward[o])
    table[128:144, 0:TERMS] = mid
    top = jnp.zeros((2, TERMS), F32)
    for o in range(8):
        top = top + nt(table[pl.ds(128 + o, 2, stride=8), :][:, :TERMS], upward[o])
    table[144:146, 0:TERMS] = top
    place = iota((1, 128), 1)
    for g in range(4):
        row = jnp.zeros((1, 128), F32)
        for c in range(4):
            row = jnp.where(place == 40 + c, tops[g, c].astype(F32), row)
        table[160 + g : 161 + g, :] = row
    mid_wide = jnp.concatenate([table[128:144, :], jnp.zeros((112, 128), F32)], axis=0)
    mid_out[...] = mid_wide.T[0:40]
    weights = []
    for a in range(3):
        values = table[...] if a == 0 else pltpu.roll(table[...], 40 * a, 1)
        high, middle, low = split3(values)
        weights.append((jnp.concatenate([high, middle], axis=1).astype(BF16), low.astype(BF16)))
    lane = iota((128, 256), 1)

    columns = jnp.concatenate([far_rows[...], mid_rows[...], jnp.zeros((108, 128), I32)], axis=0).astype(F32).T.astype(I32)

    def chosen(a, column):
        hot = jnp.where(column == lane, 1.0, 0.0).astype(BF16)
        both = jnp.dot(hot, weights[a][0], preferred_element_type=F32)
        return both[:, :128] + both[:, 128:] + jnp.dot(hot, weights[a][1], preferred_element_type=F32)

    for c in range(8):
        total = chosen(0, columns[:, c : c + 1]) + chosen(1, columns[:, c + 8 : c + 9])
        if c < 4:
            column = columns[:, 16 + c : 17 + c]
            total = total + chosen(2, jnp.where(column >= 0, column + 128, -1))
        elif c < 6:
            total = total + pltpu.roll(table[140 + c : 141 + c, :], 80, 1)
        elif c == 6:
            group = lax.shift_right_logical(iota((RANKS, 128), 0), 5)
            for g in range(4):
                total = total + jnp.where(group == g, pltpu.roll(table[160 + g : 161 + g, :], 80, 1), 0.0)
        sent[:, 32 + c, :] = total


def send_pass(near_send, tops, particles, cnt, far_rows, mid_rows, upward):
    return pl.pallas_call(
        send_kernel,
        out_shape=(
            jax.ShapeDtypeStruct((RANKS, 40, 128), F32),
            jax.ShapeDtypeStruct(((LEAVES + 1) * 8, 128), F32),
            jax.ShapeDtypeStruct((40, 128), F32),
            jax.ShapeDtypeStruct((40, 128), F32),
        ),
        in_specs=[pl.BlockSpec(memory_space=SMEM)] * 2 + [pl.BlockSpec(memory_space=VMEM)] * 5,
        out_specs=(pl.BlockSpec(memory_space=VMEM),) * 4,
        scratch_shapes=[VMEM((4, SLOTS, LEAVES), F32), VMEM((256, 128), F32)],
        compiler_params=pltpu.CompilerParams(vmem_limit_bytes=63 * MIB),
        cost_estimate=pl.CostEstimate(flops=5_000_000, bytes_accessed=2 * MIB, transcendentals=0),
        name="send_pass",
    )(near_send, tops, particles, cnt, far_rows, mid_rows, upward)


def shift_tables():
    scale = np.zeros((32, 8, 128), np.float32)
    add = np.zeros((32, 8, 128), np.float32)
    shifts = near_offsets() + [(0, 0, 0)] * 6
    for j, shift in enumerate(shifts):
        for a in range(3):
            scale[j, a] = 1.0
            scale[j, a + 4] = 1.0
            add[j, a] = 2.0 * shift[a]
            add[j, a + 4] = 2.0 * shift[a]
        add[j, 3] = 1.0
    return scale.reshape(256, 128)[:8], add.reshape(256, 128)


def source_matrix(tile, scale, add, upper):
    moved = tile * scale + add
    values = jnp.where(upper, moved, moved * moved)
    high, middle, low = split3(values)
    return jnp.concatenate([high, high, middle, high, middle, low], axis=0).astype(BF16)


def build_targets(tab, target):
    upper = iota((8, 128), 0)

    def build(i, carry):
        for l in range(8):
            b = i * 8 + l
            tile = tab[pl.ds(pl.multiple_of(b * 8, 8), 8), :]
            square = jnp.where(upper < 3, tile * tile, 0.0)
            norm = jnp.sum(square, axis=0, keepdims=True) + SOFTEN
            values = jnp.where(upper < 3, -2.0 * tile, jnp.where(upper == 3, norm, jnp.where(upper < 7, 1.0, 0.0)))
            high, middle, low = split3(values)
            wide = jnp.concatenate([high, middle, high, low, middle, high], axis=0)
            target[pl.ds(pl.multiple_of(b * 128, 128), 128), :] = wide.T.astype(BF16)
        return carry

    lax.fori_loop(0, LEAVES // 8, build, 0)


def sort_leaves(counts, order, number):
    for k in range(4):
        number[k] = 0

    def collect(i, carry):
        for n in range(8):
            b = i * 8 + n
            k = lax.shift_right_logical(counts[b] - 1, 5)
            place = number[k]
            order[k * 160 + place] = b
            number[k] = place + 1
        return carry

    lax.fori_loop(0, LEAVES // 8, collect, 0)
    for k in range(4):
        for n in range(16):
            order[k * 160 + number[k] + n] = LEAVES


def near_steps(lists, tab, add_in, scale, target, field, order, number, slots, classes, own):
    upper = iota((8, 128), 0) < 4

    def source(place, shift):
        tile = tab[pl.ds(place, 8), :]
        return source_matrix(tile, scale, add_in[pl.ds(shift, 8), :], upper), tile[3:4]

    def listed(m, b):
        word = lists[m, b]
        return source(pl.multiple_of(lax.shift_right_logical(word, 5) * 8, 8), pl.multiple_of((word & 31) * 8, 8))

    def leaf_field(word, rows, start=0):
        b = jnp.minimum(word, LEAVES - 1)
        left = target[pl.ds(pl.multiple_of(b * 128, 128), rows), :]
        picked = [listed(start + m, b) for m in range(slots)]
        if own:
            picked.append(source(pl.multiple_of(b * 8, 8), 31 * 8))
        total = None
        for p in range(0, len(picked), 2):
            (mat0, charge0), (mat1, charge1) = picked[p], picked[p + 1]
            square = jnp.dot(left, jnp.concatenate([mat0, mat1], axis=1), preferred_element_type=F32)
            second = lax.rsqrt(square[:, 128:]) * charge1
            if own and p + 2 == len(picked):
                second = jnp.where(iota((rows, 128), 0) == iota((rows, 128), 1), 0.0, second)
            term = lax.rsqrt(square[:, :128]) * charge0 + second
            total = term if total is None else total + term
        value = jnp.sum(total, axis=1, keepdims=True)
        field[0:rows, :] = jnp.where(iota((rows, 128), 1) == word, field[0:rows, :] + value, field[0:rows, :])

    for k in range(4):
        rows, together = 32 * (k + 1), classes[k]
        def work(i, carry, rows=rows, together=together, k=k):
            for n in range(together):
                leaf_field(order[k * 160 + i * together + n], rows)
            return carry

        lax.fori_loop(0, (number[k] + (together - 1)) // together, work, 0)
    return leaf_field


def near_own_kernel(lists, counts, tab, scale_in, add_in, field, target, order, number):
    field[...] = jnp.zeros((SLOTS, LEAVES), F32)
    build_targets(tab, target)
    sort_leaves(counts, order, number)
    near_steps(lists, tab, add_in, scale_in[...], target, field, order, number, OWN_SLOTS, OWN_CLASSES, True)


def near_rest_kernel(lists, order, number, extra, own, received, scale_in, add_in, target, cnt, near, far, out, field, tab):
    upper = iota((8, 128), 0) < 4
    tab[0 : 8 * (LEAVES + 1), :] = own[...]

    def build(i, carry):
        for n in range(4):
            s = i * 4 + n
            for k in range(4):
                tile = received[s, 8 * k : 8 * k + 8, :]
                turned = pltpu.roll(tile, 4, 0)
                base = pl.multiple_of(8 * (LEAVES + 1) + s * 64 + k * 16, 8)
                tab[pl.ds(base, 8), :] = jnp.where(upper, tile, turned)
                tab[pl.ds(base + 8, 8), :] = jnp.where(upper, turned, tile)
        return carry

    lax.fori_loop(0, RANKS // 4, build, 0)
    field[...] = near[...] + far[...]
    leaf_field = near_steps(lists, tab, add_in, scale_in[...], target, field, order, number, REST_SLOTS, REST_CLASSES, False)

    def more(b, carry):
        def again(c, carry):
            leaf_field(b, SLOTS, c * REST_SLOTS)
            return carry

        return lax.fori_loop(1, extra[b], again, carry)

    lax.fori_loop(0, LEAVES, more, 0)
    out[...] = jnp.where(iota((SLOTS, LEAVES), 0) < cnt[...], field[...], 0.0).T


def near_own(lists, counts, tab):
    scale, add = shift_tables()
    v = pl.BlockSpec(memory_space=VMEM)
    s = pl.BlockSpec(memory_space=SMEM)
    return pl.pallas_call(
        near_own_kernel,
        out_shape=(
            jax.ShapeDtypeStruct((SLOTS, LEAVES), F32),
            jax.ShapeDtypeStruct((LEAVES * 128, 48), BF16),
            jax.ShapeDtypeStruct((640,), I32),
            jax.ShapeDtypeStruct((8,), I32),
        ),
        in_specs=[s, s] + [v] * 3,
        out_specs=(v, v, s, s),
        compiler_params=pltpu.CompilerParams(vmem_limit_bytes=63 * MIB),
        cost_estimate=pl.CostEstimate(flops=30_000_000_000, bytes_accessed=4 * MIB, transcendentals=20_000_000),
        name="near_own",
    )(lists, counts, tab, jnp.asarray(scale), jnp.asarray(add))


def near_rest(lists, order, number, extra, tab, received, target, cnt, near, far):
    scale, add = shift_tables()
    v = pl.BlockSpec(memory_space=VMEM)
    s = pl.BlockSpec(memory_space=SMEM)
    return pl.pallas_call(
        near_rest_kernel,
        out_shape=jax.ShapeDtypeStruct((LEAVES, SLOTS), F32),
        in_specs=[s, s, s, s] + [v] * 8,
        out_specs=v,
        scratch_shapes=[
            VMEM((SLOTS, LEAVES), F32),
            VMEM((8 * (LEAVES + 1 + RANKS * 8), 128), F32),
        ],
        compiler_params=pltpu.CompilerParams(vmem_limit_bytes=63 * MIB),
        cost_estimate=pl.CostEstimate(flops=10_000_000_000, bytes_accessed=8 * MIB, transcendentals=20_000_000),
        name="near_rest",
    )(lists, order, number, extra, tab, received, jnp.asarray(scale), jnp.asarray(add), target, cnt, near, far)


def near_tables(near_lists):
    own = near_lists < LEAVES
    before = jnp.cumsum(own.astype(I32), axis=0)
    slot = jnp.arange(26, dtype=I32)[:, None]
    early = own & (before <= OWN_SLOTS)
    taken = jnp.minimum(before, OWN_SLOTS)
    empty = DUMMY * 32 + 31
    word = jnp.where(own, near_lists, near_lists + 1) * 32 + slot - empty
    tables = []
    for mine, place, size in ((early, before - 1, OWN_SLOTS), (~early, slot - taken, 3 * REST_SLOTS)):
        hits = jnp.where(mine, place, -1)[None] == jnp.arange(size, dtype=I32)[:, None, None]
        tables.append(jnp.sum(jnp.where(hits, word[None], 0), axis=1) + empty)
    goes = (26 - taken[25] + (REST_SLOTS - 1)) // REST_SLOTS
    return tables[0], tables[1], goes


N1 = sum(len(g) == 1 for g in GROUPS)
N2 = sum(len(g) == 2 for g in GROUPS)
N4 = sum(len(g) == 4 for g in GROUPS)
N8 = sum(len(g) == 8 for g in GROUPS)
MERGED = len(GROUPS)
MERGED_PAD = 192


def group_words():
    words = np.zeros((MERGED_PAD, 8), np.int32)
    for m, group in enumerate(GROUPS):
        for g in range(8):
            j, mask, value = group[min(g, len(group) - 1)]
            words[m, g] = j * 64 + mask * 8 + value
    return words


def far_kernel(
    words, where_am_i, recv, leaf, mid, far_lists, small_lists, operators, downward_in, part,
    out, rt, merged, wide, small, xs, parents, leaves, swapped,
):
    for i in range(8):
        rt[:, 128 * i : 128 * i + 128] = recv[16 * i : 16 * i + 16, 32:40, :].reshape(128, 128).T

    def two(value):
        high = value.astype(BF16).astype(F32)
        return jnp.concatenate([high, value - high], axis=0).astype(BF16)

    table = jnp.concatenate(
        [
            two(jnp.concatenate([leaf[...], rt[0:40, :]], axis=1)),
            two(jnp.concatenate([jnp.zeros((40, 128), F32), rt[40:80, :]], axis=1)),
        ],
        axis=0,
    )
    for m, group in enumerate(GROUPS):
        row = far_lists[group[0][0] : group[0][0] + 1, :]
        for j, _, _ in group[1:]:
            row = jnp.maximum(row, far_lists[j : j + 1, :])
        merged[m : m + 1, :] = row
    merged[MERGED:, :] = jnp.full((MERGED_PAD - MERGED, 128), -1, I32)
    index = merged[...]
    rel = index - LEAVES
    slot = rel & 15
    moved = lax.shift_right_logical(slot, 3) * 8192 + LEAVES + lax.shift_right_logical(rel, 4) * 8 + (slot & 7)
    merged[...] = jnp.where(rel >= 0, moved, index)
    lane = iota((40, 128), 1)

    numbers = iota((256, 384), 0).astype(F32).astype(BF16)
    one = jnp.ones((), BF16)
    zero = jnp.zeros((), BF16)

    def hot(row, depth):
        width = row.shape[1]
        upper = lax.shift_right_arithmetic(row, 8)
        lower = (row & 255).astype(F32)
        pieces = []
        for c in range((depth + 255) // 256):
            height = min(256, depth - 256 * c)
            target = jnp.broadcast_to(jnp.where(upper == c, lower, -1.0).astype(BF16), (height, width))
            number = numbers[0:height, 0:width]
            pieces.append(jnp.where(target == number, one, zero))
        return jnp.concatenate(pieces, axis=0)

    def expand(values, m, size):
        for g in range(size):
            word = words[m, g]
            j = lax.shift_right_logical(word, 6)
            keep = (lane & (lax.shift_right_logical(word, 3) & 7)) == (word & 7)
            wide[pl.ds(j, 40, stride=320), :] = jnp.where(keep, values, 0.0)

    def block(first_row, size, together):
        def body(i, carry):
            values = []
            for n in range(together):
                m = first_row + 2 * (together * i + n)
                row = jnp.concatenate([merged[pl.ds(m, 1), :], merged[pl.ds(m + 1, 1), :]], axis=1)
                late = row >= 8192
                both = jnp.dot(table, hot(jnp.where(late, row - 8192, row), 1152), preferred_element_type=F32)
                values.append((m, jnp.where(late, both[80:120] + both[120:160], both[0:40] + both[40:80])))
            for m, value in values:
                expand(value[:, :128], m, size)
                expand(value[:, 128:], m + 1, size)
            return carry

        return body

    lax.fori_loop(0, 4, block(0, 1, 13), 0)
    lax.fori_loop(0, 4, block(N1, 2, 10), 0)
    lax.fori_loop(0, 2, block(N1 + N2, 8, 4), 0)

    def contract(left, right, dims):
        lh = left.astype(BF16)
        ll = (left - lh.astype(F32)).astype(BF16)
        rh = right.astype(BF16)
        rl = (right - rh.astype(F32)).astype(BF16)
        dot = lambda a, b: lax.dot_general(a, b, (dims, ((), ())), preferred_element_type=F32)
        return dot(lh, rh) + dot(ll, rh) + dot(lh, rl)

    for level in range(3):
        swapped[level] = pltpu.einshape("ikj->kij", operators[level])
    local = jnp.zeros((TERMS, 128), F32)
    for k in range(TERMS):
        local = local + contract(swapped[0, k], wide[320 * k : 320 * k + OFFS, :], ((1,), (0,)))

    table_small = two(jnp.concatenate([mid[...], rt[80:120, :]], axis=1))
    lists = small_lists[...]
    rel = lists - 16
    mid_place = jnp.where(rel >= 0, LEAVES + lax.shift_right_logical(rel, 2) * 8 + (rel & 3), lists)
    me = where_am_i[0]
    group = lax.shift_right_logical(me, 5)
    top_place = jnp.where(lists >= 0, LEAVES + (group * 32 + lax.shift_right_arithmetic(lists, 1)) * 8 + 4 + (lists & 1), -1)
    for h in range(4):
        row = recv[h * 32 + (me & 31), 32:40, :][6:7]
        for c in range(4):
            box = row[:, 120 + c : 121 + c].astype(I32)
            place = LEAVES + (h * 32 + lax.shift_right_arithmetic(box, 1)) * 8 + 4 + (box & 1)
            top_place = jnp.where(lists == 64 + 4 * h + c, place, top_place)
    place = jnp.where(iota(lists.shape, 0) < 16, mid_place, top_place)
    for t in range(18):
        both = jnp.dot(table_small, hot(place[t : t + 1], 1152), preferred_element_type=F32)
        value = both[0:40] + both[40:80]
        for c in range(3):
            small[c, 40 * t : 40 * t + 40, :] = value[:, 128 * c : 128 * c + 128]
    mid_local = jnp.zeros((16, TERMS), F32)
    top_local = jnp.zeros((2, TERMS), F32)

    def every_40th(start, size):
        return jnp.concatenate([small[c, pl.ds(start, size, stride=40), :] for c in range(3)], axis=1)[:, :OFFS]

    for k in range(TERMS):
        dims = ((1,), (1,))
        mid_local = mid_local + contract(every_40th(k, 16), swapped[1, k], dims)
        top_local = top_local + contract(every_40th(640 + k, 2), swapped[2, k], dims)

    downward = pltpu.einshape("iok->oik", downward_in[...])
    for o in range(8):
        parents[pl.ds(o, 2, stride=8), 0:TERMS] = nt(top_local, downward[o])
    mid_total = parents[:, 0:TERMS] + mid_local
    leaves[...] = jnp.zeros((128, 128), F32)
    for o in range(8):
        leaves[pl.ds(o, 16, stride=8), 0:TERMS] = nt(mid_total, downward[o])
    leaves[...] = leaves[...].T
    leaves[0:TERMS, :] = leaves[0:TERMS, :] + local
    for a in range(3):
        xs[a] = part[a].T

    def chunk(c, carry):
        rows = pl.ds(pl.multiple_of(c * 16, 16), 16)
        basis = harmonics(xs[0, rows, :], xs[1, rows, :], xs[2, rows, :])
        total = leaves[0:1, :] * basis[0]
        for k in range(1, TERMS):
            total = total + leaves[k : k + 1, :] * basis[k]
        out[rows, :] = total
        return carry

    lax.fori_loop(0, SLOTS // 16, chunk, 0)


def far_pass(where_am_i, recv, leaf, mid, far_lists, small_lists, translate, downward, particles):
    v = pl.BlockSpec(memory_space=VMEM)
    s = pl.BlockSpec(memory_space=SMEM)
    return pl.pallas_call(
        far_kernel,
        out_shape=jax.ShapeDtypeStruct((SLOTS, LEAVES), F32),
        in_specs=[s, s] + [v] * 8,
        out_specs=v,
        scratch_shapes=[
            VMEM((128, 1024), F32),
            VMEM((MERGED_PAD, 128), I32),
            VMEM((40 * 320, 128), F32),
            VMEM((3, 18 * 40, 128), F32),
            VMEM((3, 128, 128), F32),
            VMEM((16, 128), F32),
            VMEM((128, 128), F32),
            VMEM((3, TERMS, TERMS, OFFS), F32),
        ],
        compiler_params=pltpu.CompilerParams(vmem_limit_bytes=63 * MIB),
        cost_estimate=pl.CostEstimate(flops=20_000_000_000, bytes_accessed=10 * MIB, transcendentals=0),
        name="far_pass",
    )(jnp.asarray(group_words()), where_am_i, recv, leaf, mid, far_lists, small_lists, translate, downward, particles)


def local(
    particles,
    counts,
    upward,
    downward,
    translate,
    far_send,
    mid_send,
    top_send,
    near_send,
    far_lists,
    mid_lists,
    top_lists,
    near_lists,
):
    me = lax.axis_index("group") * 32 + lax.axis_index("dev")
    cnt = counts.reshape(1, LEAVES)
    sent, tab, leaf, mid = send_pass(
        near_send[0].T, top_send[0], particles, cnt, far_send[0].T, mid_send[0].T, upward.transpose(1, 0, 2)
    )
    recv = lax.all_to_all(sent, AXES, split_axis=0, concat_axis=0, tiled=True)

    early, late, goes = near_tables(near_lists)
    small_lists = jnp.pad(jnp.concatenate([mid_lists, top_lists], axis=1).T, ((0, 6), (0, 68)), constant_values=-1)
    near, target, order, number = near_own(early, counts, tab)
    far = far_pass(me.reshape(1), recv, leaf, mid, far_lists, small_lists, translate, downward.transpose(1, 0, 2), particles)
    return near_rest(late, order, number, goes, tab, recv, target, cnt, near, far)


def solution(mesh):
    in_specs = (
        P(None, AXES, None),
        P(AXES),
        P(),
        P(),
        P(),
        P(AXES, None, None),
        P(AXES, None, None),
        P(AXES, None, None),
        P(AXES, None, None),
        P(None, AXES),
        P(None, AXES),
        P(None, AXES),
        P(None, AXES),
    )
    return jax.shard_map(local, mesh=mesh, in_specs=in_specs, out_specs=P(AXES, None), check_vma=False)
```

```python
import math

import jax
import jax.numpy as jnp
import numpy as np
from jax import lax
from jax.experimental import pallas as pl
from jax.experimental.pallas import tpu as pltpu
from jax.sharding import PartitionSpec as P

ORDER = 6
TERMS = 36
OFFS = 316
SOFTEN = 0.01
LEAVES = 128
SLOTS = 128
RANKS = 128
AXES = ("group", "dev")
F32 = jnp.float32
BF16 = jnp.bfloat16
I32 = jnp.int32
HIGH = lax.Precision.HIGHEST
VMEM = pltpu.VMEM
SMEM = pltpu.SMEM
MIB = 1 << 20
OWN_SLOTS = 17
REST_SLOTS = 10
DUMMY = LEAVES
OWN_CLASSES = (11, 8, 6, 6)
REST_CLASSES = (16, 11, 11, 11)


def harmonics(coord_x, coord_y, coord_z):
    radius_sq = coord_x * coord_x + coord_y * coord_y + coord_z * coord_z
    real_part = {(0, 0): jnp.ones_like(coord_x)}
    imag_part = {}
    for degree in range(1, ORDER):
        scale = 1.0 / (2.0 * degree)
        if degree == 1:
            real_part[1, 1] = coord_x * scale
            imag_part[1, 1] = coord_y * scale
        else:
            prior_re = real_part[degree - 1, degree - 1]
            prior_im = imag_part[degree - 1, degree - 1]
            real_part[degree, degree] = (coord_x * prior_re - coord_y * prior_im) * scale
            imag_part[degree, degree] = (coord_x * prior_im + coord_y * prior_re) * scale
        for column in range(degree):
            factor = 1.0 / ((degree + column) * (degree - column))
            lead = ((2.0 * degree - 1.0) * factor) * coord_z
            for part in (real_part, imag_part):
                if (degree - 1, column) not in part:
                    continue
                value = lead * part[degree - 1, column]
                if column <= degree - 2:
                    value = value - (radius_sq * factor) * part[degree - 2, column]
                part[degree, column] = value
    pieces = []
    for degree in range(ORDER):
        for column in range(degree + 1):
            weight = math.sqrt(math.factorial(degree - column) * math.factorial(degree + column))
            pieces.append(weight * real_part[degree, column])
            if column > 0:
                pieces.append(weight * imag_part[degree, column])
    return pieces


def near_offsets():
    shifts = []
    for step_x in (-1, 0, 1):
        for step_y in (-1, 0, 1):
            for step_z in (-1, 0, 1):
                if step_x != 0 or step_y != 0 or step_z != 0:
                    shifts.append((step_x, step_y, step_z))
    return shifts


def far_groups():
    offsets = []
    for step_x in range(-3, 4):
        for step_y in range(-3, 4):
            for step_z in range(-3, 4):
                if max(abs(step_x), abs(step_y), abs(step_z)) >= 2:
                    offsets.append((step_x, step_y, step_z))
    groups = {}
    for j, offset in enumerate(offsets):
        mask, value = 0, 0
        for axis in range(3):
            if abs(offset[axis]) == 3:
                mask |= 1 << axis
                if offset[axis] == -3:
                    value |= 1 << axis
        key = tuple(abs(v) if abs(v) == 3 else v for v in offset)
        groups.setdefault(key, []).append((j, mask, value))
    return sorted(groups.values(), key=len)


GROUPS = far_groups()


def split3(value):
    high = value.astype(BF16).astype(F32)
    rest = value - high
    mid = rest.astype(BF16).astype(F32)
    return high, mid, rest - mid


def iota(shape, dim):
    return lax.broadcasted_iota(I32, shape, dim)


def nt(left, right):
    return lax.dot_general(left, right, (((1,), (1,)), ((), ())), precision=HIGH, preferred_element_type=F32)


def send_kernel(near_send, tops, part, cnt, far_rows, mid_rows, upward_in, sent, tab, leaf_out, mid_out, xs, table):
    filled = iota((SLOTS, LEAVES), 0) < cnt[...]
    for a in range(3):
        xs[a] = part[a].T
    xs[3] = jnp.where(filled, part[3].T, 0.0)
    comps = [part[0], part[1], part[2], xs[3].T]
    for a in range(4):
        tab[pl.ds(a, LEAVES, stride=8), :] = comps[a]
        tab[pl.ds(a + 4, LEAVES, stride=8), :] = comps[a]
    tab[8 * DUMMY : 8 * DUMMY + 8, :] = jnp.zeros((8, 128), F32)
    upper = iota((8, 128), 0) < 4

    def pack(i, carry):
        for n in range(4):
            r = i * 4 + n
            for k in range(4):
                first = jnp.maximum(near_send[2 * k, r], 0)
                second = jnp.maximum(near_send[2 * k + 1, r], 0)
                tile0 = tab[pl.ds(pl.multiple_of(first * 8, 8), 8), :]
                tile1 = tab[pl.ds(pl.multiple_of(second * 8, 8), 8), :]
                sent[r, 8 * k : 8 * k + 8, :] = jnp.where(upper, tile0, tile1)
        return carry

    lax.fori_loop(0, RANKS // 4, pack, 0)

    def chunk(c, acc):
        rows = pl.ds(pl.multiple_of(c * 16, 16), 16)
        charge = xs[3, rows, :]
        basis = harmonics(xs[0, rows, :], xs[1, rows, :], xs[2, rows, :])
        terms = [charge * value for value in basis]
        return tuple(old + (term[0:8] + term[8:16]) for old, term in zip(acc, terms))

    zero = jnp.zeros((8, 128), F32)
    acc = lax.fori_loop(0, SLOTS // 16, chunk, (zero,) * TERMS)
    rows = [jnp.sum(value, axis=0, keepdims=True) for value in acc]
    leaf = jnp.concatenate(rows + [jnp.zeros((4, 128), F32)], axis=0)
    leaf_out[...] = leaf
    table[...] = jnp.zeros((256, 128), F32)
    table[0:128, :] = jnp.concatenate([leaf, jnp.zeros((88, 128), F32)], axis=0).T
    upward = pltpu.einshape("iok->oik", upward_in[...])
    mid = jnp.zeros((16, TERMS), F32)
    for o in range(8):
        mid = mid + nt(table[pl.ds(o, 16, stride=8), :][:, :TERMS], upward[o])
    table[128:144, 0:TERMS] = mid
    top = jnp.zeros((2, TERMS), F32)
    for o in range(8):
        top = top + nt(table[pl.ds(128 + o, 2, stride=8), :][:, :TERMS], upward[o])
    table[144:146, 0:TERMS] = top
    place = iota((1, 128), 1)
    for g in range(4):
        row = jnp.zeros((1, 128), F32)
        for c in range(4):
            row = jnp.where(place == 40 + c, tops[g, c].astype(F32), row)
        table[160 + g : 161 + g, :] = row
    mid_wide = jnp.concatenate([table[128:144, :], jnp.zeros((112, 128), F32)], axis=0)
    mid_out[...] = mid_wide.T[0:40]
    weights = []
    for a in range(3):
        values = table[...] if a == 0 else pltpu.roll(table[...], 40 * a, 1)
        high, middle, low = split3(values)
        weights.append((jnp.concatenate([high, middle], axis=1).astype(BF16), low.astype(BF16)))
    lane = iota((128, 256), 1)

    columns = jnp.concatenate([far_rows[...], mid_rows[...], jnp.zeros((108, 128), I32)], axis=0).astype(F32).T.astype(I32)

    def chosen(a, column):
        hot = jnp.where(column == lane, 1.0, 0.0).astype(BF16)
        both = jnp.dot(hot, weights[a][0], preferred_element_type=F32)
        return both[:, :128] + both[:, 128:] + jnp.dot(hot, weights[a][1], preferred_element_type=F32)

    for c in range(8):
        total = chosen(0, columns[:, c : c + 1]) + chosen(1, columns[:, c + 8 : c + 9])
        if c < 4:
            column = columns[:, 16 + c : 17 + c]
            total = total + chosen(2, jnp.where(column >= 0, column + 128, -1))
        elif c < 6:
            total = total + pltpu.roll(table[140 + c : 141 + c, :], 80, 1)
        elif c == 6:
            group = lax.shift_right_logical(iota((RANKS, 128), 0), 5)
            for g in range(4):
                total = total + jnp.where(group == g, pltpu.roll(table[160 + g : 161 + g, :], 80, 1), 0.0)
        sent[:, 32 + c, :] = total


def send_pass(near_send, tops, particles, cnt, far_rows, mid_rows, upward):
    return pl.pallas_call(
        send_kernel,
        out_shape=(
            jax.ShapeDtypeStruct((RANKS, 40, 128), F32),
            jax.ShapeDtypeStruct(((LEAVES + 1) * 8, 128), F32),
            jax.ShapeDtypeStruct((40, 128), F32),
            jax.ShapeDtypeStruct((40, 128), F32),
        ),
        in_specs=[pl.BlockSpec(memory_space=SMEM)] * 2 + [pl.BlockSpec(memory_space=VMEM)] * 5,
        out_specs=(pl.BlockSpec(memory_space=VMEM),) * 4,
        scratch_shapes=[VMEM((4, SLOTS, LEAVES), F32), VMEM((256, 128), F32)],
        compiler_params=pltpu.CompilerParams(vmem_limit_bytes=63 * MIB),
        cost_estimate=pl.CostEstimate(flops=5_000_000, bytes_accessed=2 * MIB, transcendentals=0),
        name="send_pass",
    )(near_send, tops, particles, cnt, far_rows, mid_rows, upward)


def shift_tables():
    scale = np.zeros((32, 8, 128), np.float32)
    add = np.zeros((32, 8, 128), np.float32)
    shifts = near_offsets() + [(0, 0, 0)] * 6
    for j, shift in enumerate(shifts):
        for a in range(3):
            scale[j, a] = 1.0
            scale[j, a + 4] = 1.0
            add[j, a] = 2.0 * shift[a]
            add[j, a + 4] = 2.0 * shift[a]
        add[j, 3] = 1.0
    return scale.reshape(256, 128)[:8], add.reshape(256, 128)


def source_matrix(tile, scale, add, upper):
    moved = tile * scale + add
    values = jnp.where(upper, moved, moved * moved)
    high, middle, low = split3(values)
    return jnp.concatenate([high, high, middle, high, middle, low], axis=0).astype(BF16)


def build_targets(tab, target):
    upper = iota((8, 128), 0)

    def build(i, carry):
        for l in range(8):
            b = i * 8 + l
            tile = tab[pl.ds(pl.multiple_of(b * 8, 8), 8), :]
            square = jnp.where(upper < 3, tile * tile, 0.0)
            norm = jnp.sum(square, axis=0, keepdims=True) + SOFTEN
            values = jnp.where(upper < 3, -2.0 * tile, jnp.where(upper == 3, norm, jnp.where(upper < 7, 1.0, 0.0)))
            high, middle, low = split3(values)
            wide = jnp.concatenate([high, middle, high, low, middle, high], axis=0)
            target[pl.ds(pl.multiple_of(b * 128, 128), 128), :] = wide.T.astype(BF16)
        return carry

    lax.fori_loop(0, LEAVES // 8, build, 0)


def sort_leaves(counts, order, number):
    for k in range(4):
        number[k] = 0

    def collect(i, carry):
        for n in range(8):
            b = i * 8 + n
            k = lax.shift_right_logical(counts[b] - 1, 5)
            place = number[k]
            order[k * 160 + place] = b
            number[k] = place + 1
        return carry

    lax.fori_loop(0, LEAVES // 8, collect, 0)
    for k in range(4):
        for n in range(16):
            order[k * 160 + number[k] + n] = LEAVES


def near_steps(lists, tab, add_in, scale, target, field, order, number, slots, classes, own):
    upper = iota((8, 128), 0) < 4

    def source(place, shift):
        tile = tab[pl.ds(place, 8), :]
        return source_matrix(tile, scale, add_in[pl.ds(shift, 8), :], upper), tile[3:4]

    def listed(m, b):
        word = lists[m, b]
        return source(pl.multiple_of(lax.shift_right_logical(word, 5) * 8, 8), pl.multiple_of((word & 31) * 8, 8))

    def leaf_field(word, rows, start=0):
        b = jnp.minimum(word, LEAVES - 1)
        left = target[pl.ds(pl.multiple_of(b * 128, 128), rows), :]
        picked = [listed(start + m, b) for m in range(slots)]
        if own:
            picked.append(source(pl.multiple_of(b * 8, 8), 31 * 8))
        total = None
        for p in range(0, len(picked), 2):
            (mat0, charge0), (mat1, charge1) = picked[p], picked[p + 1]
            square = jnp.dot(left, jnp.concatenate([mat0, mat1], axis=1), preferred_element_type=F32)
            second = lax.rsqrt(square[:, 128:]) * charge1
            if own and p + 2 == len(picked):
                second = jnp.where(iota((rows, 128), 0) == iota((rows, 128), 1), 0.0, second)
            term = lax.rsqrt(square[:, :128]) * charge0 + second
            total = term if total is None else total + term
        value = jnp.sum(total, axis=1, keepdims=True)
        field[0:rows, :] = jnp.where(iota((rows, 128), 1) == word, field[0:rows, :] + value, field[0:rows, :])

    for k in range(4):
        rows, together = 32 * (k + 1), classes[k]
        def work(i, carry, rows=rows, together=together, k=k):
            for n in range(together):
                leaf_field(order[k * 160 + i * together + n], rows)
            return carry

        lax.fori_loop(0, (number[k] + (together - 1)) // together, work, 0)
    return leaf_field


def near_own_kernel(lists, counts, tab, scale_in, add_in, field, target, order, number):
    field[...] = jnp.zeros((SLOTS, LEAVES), F32)
    build_targets(tab, target)
    sort_leaves(counts, order, number)
    near_steps(lists, tab, add_in, scale_in[...], target, field, order, number, OWN_SLOTS, OWN_CLASSES, True)


def near_rest_kernel(lists, order, number, extra, own, received, scale_in, add_in, target_in, cnt, near, far, out, field, tab, target, arrived):
    upper = iota((8, 128), 0) < 4
    fetch = pltpu.make_async_copy(target_in, target, arrived)
    fetch.start()
    tab[0 : 8 * (LEAVES + 1), :] = own[...]

    def build(i, carry):
        for n in range(4):
            s = i * 4 + n
            for k in range(4):
                tile = received[s, 8 * k : 8 * k + 8, :]
                turned = pltpu.roll(tile, 4, 0)
                base = pl.multiple_of(8 * (LEAVES + 1) + s * 64 + k * 16, 8)
                tab[pl.ds(base, 8), :] = jnp.where(upper, tile, turned)
                tab[pl.ds(base + 8, 8), :] = jnp.where(upper, turned, tile)
        return carry

    lax.fori_loop(0, RANKS // 4, build, 0)
    field[...] = near[...] + far[...]
    fetch.wait()
    leaf_field = near_steps(lists, tab, add_in, scale_in[...], target, field, order, number, REST_SLOTS, REST_CLASSES, False)

    def more(b, carry):
        def again(c, carry):
            leaf_field(b, SLOTS, c * REST_SLOTS)
            return carry

        return lax.fori_loop(1, extra[b], again, carry)

    lax.fori_loop(0, LEAVES, more, 0)
    out[...] = jnp.where(iota((SLOTS, LEAVES), 0) < cnt[...], field[...], 0.0).T


def near_own(lists, counts, tab):
    scale, add = shift_tables()
    v = pl.BlockSpec(memory_space=VMEM)
    s = pl.BlockSpec(memory_space=SMEM)
    return pl.pallas_call(
        near_own_kernel,
        out_shape=(
            jax.ShapeDtypeStruct((SLOTS, LEAVES), F32),
            jax.ShapeDtypeStruct((LEAVES * 128, 48), BF16),
            jax.ShapeDtypeStruct((640,), I32),
            jax.ShapeDtypeStruct((8,), I32),
        ),
        in_specs=[s, s] + [v] * 3,
        out_specs=(v, v, s, s),
        compiler_params=pltpu.CompilerParams(vmem_limit_bytes=63 * MIB),
        cost_estimate=pl.CostEstimate(flops=30_000_000_000, bytes_accessed=4 * MIB, transcendentals=20_000_000),
        name="near_own",
    )(lists, counts, tab, jnp.asarray(scale), jnp.asarray(add))


def near_rest(lists, order, number, extra, tab, received, target, cnt, near, far):
    scale, add = shift_tables()
    v = pl.BlockSpec(memory_space=VMEM)
    s = pl.BlockSpec(memory_space=SMEM)
    return pl.pallas_call(
        near_rest_kernel,
        out_shape=jax.ShapeDtypeStruct((LEAVES, SLOTS), F32),
        in_specs=[s, s, s, s] + [v] * 4 + [pl.BlockSpec(memory_space=pl.ANY)] + [v] * 3,
        out_specs=v,
        scratch_shapes=[
            VMEM((SLOTS, LEAVES), F32),
            VMEM((8 * (LEAVES + 1 + RANKS * 8), 128), F32),
            VMEM((LEAVES * 128, 48), BF16),
            pltpu.SemaphoreType.DMA,
        ],
        compiler_params=pltpu.CompilerParams(vmem_limit_bytes=63 * MIB),
        cost_estimate=pl.CostEstimate(flops=10_000_000_000, bytes_accessed=8 * MIB, transcendentals=20_000_000),
        name="near_rest",
    )(lists, order, number, extra, tab, received, jnp.asarray(scale), jnp.asarray(add), target, cnt, near, far)


def near_tables(near_lists):
    own = near_lists < LEAVES
    before = jnp.cumsum(own.astype(I32), axis=0)
    slot = jnp.arange(26, dtype=I32)[:, None]
    early = own & (before <= OWN_SLOTS)
    taken = jnp.minimum(before, OWN_SLOTS)
    empty = DUMMY * 32 + 31
    word = jnp.where(own, near_lists, near_lists + 1) * 32 + slot - empty
    tables = []
    for mine, place, size in ((early, before - 1, OWN_SLOTS), (~early, slot - taken, 3 * REST_SLOTS)):
        hits = jnp.where(mine, place, -1)[None] == jnp.arange(size, dtype=I32)[:, None, None]
        tables.append(jnp.sum(jnp.where(hits, word[None], 0), axis=1) + empty)
    goes = (26 - taken[25] + (REST_SLOTS - 1)) // REST_SLOTS
    return tables[0], tables[1], goes


N1 = sum(len(g) == 1 for g in GROUPS)
N2 = sum(len(g) == 2 for g in GROUPS)
N4 = sum(len(g) == 4 for g in GROUPS)
N8 = sum(len(g) == 8 for g in GROUPS)
MERGED = len(GROUPS)
MERGED_PAD = 192
WIDE = 321


def group_words():
    words = np.zeros((MERGED_PAD, 8), np.int32)
    for m, group in enumerate(GROUPS):
        for g in range(8):
            j, mask, value = group[min(g, len(group) - 1)]
            words[m, g] = j * 64 + mask * 8 + value
    return words


def far_kernel(
    words, where_am_i, recv, leaf, mid, far_lists, small_lists, operators_in, downward_in, part,
    out, rt, merged, wide, small, xs, parents, leaves, swapped, operators, arrived,
):
    fetch = pltpu.make_async_copy(operators_in, operators, arrived)
    fetch.start()
    for i in range(8):
        rt[:, 128 * i : 128 * i + 128] = recv[16 * i : 16 * i + 16, 32:40, :].reshape(128, 128).T

    def two(value):
        high = value.astype(BF16).astype(F32)
        return jnp.concatenate([high, value - high], axis=0).astype(BF16)

    table = jnp.concatenate(
        [
            two(jnp.concatenate([leaf[...], rt[0:40, :]], axis=1)),
            two(jnp.concatenate([jnp.zeros((40, 128), F32), rt[40:80, :]], axis=1)),
        ],
        axis=0,
    )
    for m, group in enumerate(GROUPS):
        row = far_lists[group[0][0] : group[0][0] + 1, :]
        for j, _, _ in group[1:]:
            row = jnp.maximum(row, far_lists[j : j + 1, :])
        merged[m : m + 1, :] = row
    merged[MERGED:, :] = jnp.full((MERGED_PAD - MERGED, 128), -1, I32)
    index = merged[...]
    rel = index - LEAVES
    slot = rel & 15
    moved = lax.shift_right_logical(slot, 3) * 8192 + LEAVES + lax.shift_right_logical(rel, 4) * 8 + (slot & 7)
    merged[...] = jnp.where(rel >= 0, moved, index)
    lane = iota((40, 128), 1)

    numbers = iota((256, 384), 0).astype(F32).astype(BF16)
    one = jnp.ones((), BF16)
    zero = jnp.zeros((), BF16)

    def hot(row, depth):
        width = row.shape[1]
        upper = lax.shift_right_arithmetic(row, 8)
        lower = (row & 255).astype(F32)
        pieces = []
        for c in range((depth + 255) // 256):
            height = min(256, depth - 256 * c)
            target = jnp.broadcast_to(jnp.where(upper == c, lower, -1.0).astype(BF16), (height, width))
            number = numbers[0:height, 0:width]
            pieces.append(jnp.where(target == number, one, zero))
        return jnp.concatenate(pieces, axis=0)

    def expand(values, m, size):
        for g in range(size):
            word = words[m, g]
            j = lax.shift_right_logical(word, 6)
            keep = (lane & (lax.shift_right_logical(word, 3) & 7)) == (word & 7)
            wide[pl.ds(j, 40, stride=WIDE), :] = jnp.where(keep, values, 0.0)

    def block(first_row, size, together):
        def body(i, carry):
            values = []
            for n in range(together):
                m = first_row + 2 * (together * i + n)
                row = jnp.concatenate([merged[pl.ds(m, 1), :], merged[pl.ds(m + 1, 1), :]], axis=1)
                late = row >= 8192
                both = jnp.dot(table, hot(jnp.where(late, row - 8192, row), 1152), preferred_element_type=F32)
                values.append((m, jnp.where(late, both[80:120] + both[120:160], both[0:40] + both[40:80])))
            for m, value in values:
                expand(value[:, :128], m, size)
                expand(value[:, 128:], m + 1, size)
            return carry

        return body

    lax.fori_loop(0, 4, block(0, 1, 13), 0)
    lax.fori_loop(0, 4, block(N1, 2, 10), 0)
    lax.fori_loop(0, 2, block(N1 + N2, 8, 4), 0)

    def contract(left, right, dims):
        lh = left.astype(BF16)
        ll = (left - lh.astype(F32)).astype(BF16)
        rh = right.astype(BF16)
        rl = (right - rh.astype(F32)).astype(BF16)
        dot = lambda a, b: lax.dot_general(a, b, (dims, ((), ())), preferred_element_type=F32)
        return dot(lh, rh) + dot(ll, rh) + dot(lh, rl)

    fetch.wait()
    for level in range(3):
        swapped[level] = pltpu.einshape("ikj->kij", operators[level])
    local = jnp.zeros((TERMS, 128), F32)
    for k in range(TERMS):
        local = local + contract(swapped[0, k], wide[WIDE * k : WIDE * k + OFFS, :], ((1,), (0,)))

    table_small = two(jnp.concatenate([mid[...], rt[80:120, :]], axis=1))
    lists = small_lists[...]
    rel = lists - 16
    mid_place = jnp.where(rel >= 0, LEAVES + lax.shift_right_logical(rel, 2) * 8 + (rel & 3), lists)
    me = where_am_i[0]
    group = lax.shift_right_logical(me, 5)
    top_place = jnp.where(lists >= 0, LEAVES + (group * 32 + lax.shift_right_arithmetic(lists, 1)) * 8 + 4 + (lists & 1), -1)
    for h in range(4):
        row = recv[h * 32 + (me & 31), 32:40, :][6:7]
        for c in range(4):
            box = row[:, 120 + c : 121 + c].astype(I32)
            place = LEAVES + (h * 32 + lax.shift_right_arithmetic(box, 1)) * 8 + 4 + (box & 1)
            top_place = jnp.where(lists == 64 + 4 * h + c, place, top_place)
    place = jnp.where(iota(lists.shape, 0) < 16, mid_place, top_place)
    for t in range(18):
        both = jnp.dot(table_small, hot(place[t : t + 1], 1152), preferred_element_type=F32)
        value = both[0:40] + both[40:80]
        for c in range(3):
            small[c, 40 * t : 40 * t + 40, :] = value[:, 128 * c : 128 * c + 128]
    mid_local = jnp.zeros((16, TERMS), F32)
    top_local = jnp.zeros((2, TERMS), F32)

    def every_40th(start, size):
        return jnp.concatenate([small[c, pl.ds(start, size, stride=40), :] for c in range(3)], axis=1)[:, :OFFS]

    for k in range(TERMS):
        dims = ((1,), (1,))
        mid_local = mid_local + contract(every_40th(k, 16), swapped[1, k], dims)
        top_local = top_local + contract(every_40th(640 + k, 2), swapped[2, k], dims)

    downward = pltpu.einshape("iok->oik", downward_in[...])
    for o in range(8):
        parents[pl.ds(o, 2, stride=8), 0:TERMS] = nt(top_local, downward[o])
    mid_total = parents[:, 0:TERMS] + mid_local
    leaves[...] = jnp.zeros((128, 128), F32)
    for o in range(8):
        leaves[pl.ds(o, 16, stride=8), 0:TERMS] = nt(mid_total, downward[o])
    leaves[...] = leaves[...].T
    leaves[0:TERMS, :] = leaves[0:TERMS, :] + local
    for a in range(3):
        xs[a] = part[a].T

    def chunk(c, carry):
        rows = pl.ds(pl.multiple_of(c * 16, 16), 16)
        basis = harmonics(xs[0, rows, :], xs[1, rows, :], xs[2, rows, :])
        total = leaves[0:1, :] * basis[0]
        for k in range(1, TERMS):
            total = total + leaves[k : k + 1, :] * basis[k]
        out[rows, :] = total
        return carry

    lax.fori_loop(0, SLOTS // 16, chunk, 0)


def far_pass(where_am_i, recv, leaf, mid, far_lists, small_lists, translate, downward, particles):
    v = pl.BlockSpec(memory_space=VMEM)
    s = pl.BlockSpec(memory_space=SMEM)
    return pl.pallas_call(
        far_kernel,
        out_shape=jax.ShapeDtypeStruct((SLOTS, LEAVES), F32),
        in_specs=[s, s] + [v] * 5 + [pl.BlockSpec(memory_space=pl.ANY)] + [v] * 2,
        out_specs=v,
        scratch_shapes=[
            VMEM((128, 1024), F32),
            VMEM((MERGED_PAD, 128), I32),
            VMEM((40 * WIDE, 128), F32),
            VMEM((3, 18 * 40, 128), F32),
            VMEM((3, 128, 128), F32),
            VMEM((16, 128), F32),
            VMEM((128, 128), F32),
            VMEM((3, TERMS, TERMS, OFFS), F32),
            VMEM((3, TERMS, TERMS, OFFS), F32),
            pltpu.SemaphoreType.DMA,
        ],
        compiler_params=pltpu.CompilerParams(vmem_limit_bytes=63 * MIB),
        cost_estimate=pl.CostEstimate(flops=20_000_000_000, bytes_accessed=10 * MIB, transcendentals=0),
        name="far_pass",
    )(jnp.asarray(group_words()), where_am_i, recv, leaf, mid, far_lists, small_lists, translate, downward, particles)


def local(
    particles,
    counts,
    upward,
    downward,
    translate,
    far_send,
    mid_send,
    top_send,
    near_send,
    far_lists,
    mid_lists,
    top_lists,
    near_lists,
):
    me = lax.axis_index("group") * 32 + lax.axis_index("dev")
    cnt = counts.reshape(1, LEAVES)
    sent, tab, leaf, mid = send_pass(
        near_send[0].T, top_send[0], particles, cnt, far_send[0].T, mid_send[0].T, upward.transpose(1, 0, 2)
    )
    recv = lax.all_to_all(sent, AXES, split_axis=0, concat_axis=0, tiled=True)

    early, late, goes = near_tables(near_lists)
    small_lists = jnp.pad(jnp.concatenate([mid_lists, top_lists], axis=1).T, ((0, 6), (0, 68)), constant_values=-1)
    near, target, order, number = near_own(early, counts, tab)
    far = far_pass(me.reshape(1), recv, leaf, mid, far_lists, small_lists, translate, downward.transpose(1, 0, 2), particles)
    return near_rest(late, order, number, goes, tab, recv, target, cnt, near, far)


def solution(mesh):
    in_specs = (
        P(None, AXES, None),
        P(AXES),
        P(),
        P(),
        P(),
        P(AXES, None, None),
        P(AXES, None, None),
        P(AXES, None, None),
        P(AXES, None, None),
        P(None, AXES),
        P(None, AXES),
        P(None, AXES),
        P(None, AXES),
    )
    return jax.shard_map(local, mesh=mesh, in_specs=in_specs, out_specs=P(AXES, None), check_vma=False)
```
